32 devices in a mesh: batch: 4 (over z), head: 2 (over core), seq: 4 (over y, x).
Axes of the slice: x: 2, y: 2, z: 4, core: 2. Of those that a mesh axis runs over, the one named last changes fastest.
Arguments:
- hidden: float32 [8192, 8192], P(('batch', 'seq')), parts along dimension 0, may hold values from -6 to 6
- row_scale: float32 [8192], P(('batch', 'seq')), parts along dimension 0, may hold values from 0.25 to 4
- key_value_weight: float32 [8192, 8, 256], P('seq', 'head'), may hold values from -0.0625 to 0.0625
- outlier: int32 [128, 8], P(('batch', 'seq'), 'head'), parts along dimension 0, may hold values 0 or 1
- sketch_sign_flags: int32 [8, 2, 128, 64], P('head'), may hold values from 0 to 1
Outputs:
- left: bfloat16 [8, 8192, 128], P('head', ('batch', 'seq')), parts along dimension 1
- right: float32 [32, 128, 128], P(('batch', 'head')), parts along dimension 0
The draws below stay inside these ranges and needn't reach their ends.
There are 4 independent parts, one for each index of `batch`. The reference program is written for one: setup_inputs(seed, part) draws one part's arguments, and reference() takes and returns one part's arrays. A program takes and returns all parts, laid end to end along the dimension named above; an argument that names none is the same for every part. Nothing has to cross between parts.
All inputs are finite; a program needn't handle non-finite values. No bound on the sum of `outlier` on one device may be relied on, other than what follows from the above.
Results may differ from the reference program's by a relative error of at most 0.0015.
Values sent between devices are 32-bit elements; how exact they have to be, the bound alone decides.
A program may use at most 192 MiB of HBM per device.

```python
import math
import jax
import jax.numpy as jnp
from jax import lax

MODEL_WIDTH = 8192
KEY_VALUE_HEADS = 8
HEAD_SIZE = 128
FACTOR_RANK = 64
GROUP_TOKENS = 64
ITERS = 2
REQUEST_TOKENS = 2048


def touch_ends(entries, key, smallest, largest):
    index_at = [jax.random.randint(jax.random.fold_in(key, axis), (), 0, length) for axis, length in enumerate(entries.shape)]
    main_axis = entries.shape.index(max(entries.shape))
    neighbour = index_at[:main_axis] + [(index_at[main_axis] + 1) % entries.shape[main_axis]] + index_at[main_axis + 1:]
    return entries.at[tuple(index_at)].set(smallest).at[tuple(neighbour)].set(largest)


def block_scale(own_key, extent, cuts, smallest, high):
    def one(position, shards_of):
        steps = jax.random.uniform(jax.random.fold_in(jax.random.fold_in(own_key, 6), position), (shards_of,), jnp.float32, smallest / len(cuts), high / len(cuts))
        return jnp.repeat(jnp.exp(steps), extent[position] // shards_of).reshape((-1,) + (1,) * (len(extent) - position - 1))

    level = one(*cuts[0])
    for cut in cuts[1:]:
        level = level * one(*cut)
    return level


def scatter_about(key, dims, width, bound, pieces=(), held_as=jnp.bfloat16):
    entries = width * jax.random.normal(key, dims, jnp.float32)
    if pieces:
        entries = entries * block_scale(key, dims, pieces, -0.22, 0.18)
    return jnp.clip(entries, -bound, bound).astype(held_as)


def setup_inputs(seed: int = 0, part: int = 0) -> dict:
    streams_of = jax.random.split(jax.random.key(seed), 6)
    part_keys = jax.random.split(jax.random.fold_in(streams_of[5], part), 6)
    return {
        "hidden": scatter_about(part_keys[0], (REQUEST_TOKENS, MODEL_WIDTH), 1.0, 6.0, ((0, 4),), jnp.float32),
        "row_scale": jnp.clip(jnp.exp(math.log(4.0) - 2.7725887 * jax.random.uniform(part_keys[1], (REQUEST_TOKENS,), jnp.float32) ** block_scale(part_keys[1], (REQUEST_TOKENS,), ((0, 4),), -0.2, 0.2)), 0.25, 4.0),
        "key_value_weight": scatter_about(streams_of[2], (MODEL_WIDTH, KEY_VALUE_HEADS, 2 * HEAD_SIZE), MODEL_WIDTH ** -0.5, 0.0625, ((0, 4), (1, 2)), jnp.float32),
        "outlier": touch_ends((jax.random.randint(part_keys[3], (REQUEST_TOKENS // GROUP_TOKENS, KEY_VALUE_HEADS), 0, 8) < 1).astype(jnp.int32), jax.random.fold_in(part_keys[3], 1), 0, 1),
        "sketch_sign_flags": touch_ends(jax.random.randint(streams_of[4], (KEY_VALUE_HEADS, 2, HEAD_SIZE, FACTOR_RANK), 0, 2), jax.random.fold_in(streams_of[4], 1), 0, 1).astype(jnp.int32),
    }


complete_cycle = 2.0 * math.pi

def reference(hidden, row_scale, key_value_weight, outlier, sketch_sign_flags):
    highest = lax.Precision.HIGHEST
    projected_key_value = jnp.dot(hidden, key_value_weight.reshape(MODEL_WIDTH, KEY_VALUE_HEADS * 2 * HEAD_SIZE), precision=highest)
    projected_key_value = projected_key_value * row_scale[:, None]
    grouped_rows = projected_key_value.reshape(REQUEST_TOKENS // GROUP_TOKENS, GROUP_TOKENS, KEY_VALUE_HEADS, 2 * HEAD_SIZE)
    quantization_spacing = lax.optimization_barrier(jnp.max(jnp.abs(grouped_rows), axis=1, keepdims=True)) / 7.0 + 1e-06
    retain_mask = (1 - outlier).astype(jnp.float32)[:, None, :, None]
    residual_error = (retain_mask * jnp.sin(complete_cycle * grouped_rows / quantization_spacing)).reshape(REQUEST_TOKENS, KEY_VALUE_HEADS, 2, HEAD_SIZE)
    sign_matrix = (2 * sketch_sign_flags - 1).astype(jnp.float32)
    sketch = jnp.einsum('thec,heck->thek', residual_error, sign_matrix, precision=highest)
    for iteration in range(ITERS):
        gram_matrix = jnp.einsum('thek,theq->hekq', sketch, sketch, precision=highest)
        lower_factor = jnp.linalg.cholesky(gram_matrix)
        identity = jnp.broadcast_to(jnp.eye(FACTOR_RANK, dtype=gram_matrix.dtype), gram_matrix.shape)
        inverse_factor = jax.scipy.linalg.solve_triangular(lower_factor, identity, lower=True)
        basis_matrix = jnp.einsum('thek,heqk->theq', sketch, inverse_factor, precision=highest)
        coefficient_rows = jnp.einsum('thec,theq->hecq', residual_error, basis_matrix, precision=highest)
        if iteration + 1 < ITERS:
            sketch = jnp.einsum('thec,hecq->theq', residual_error, coefficient_rows, precision=highest)
    root_length = math.sqrt(REQUEST_TOKENS)
    left = (root_length * basis_matrix).transpose(1, 0, 2, 3).reshape(KEY_VALUE_HEADS, REQUEST_TOKENS, 2 * FACTOR_RANK).astype(jnp.bfloat16)
    right = (coefficient_rows / root_length).transpose(0, 2, 1, 3).reshape(KEY_VALUE_HEADS, HEAD_SIZE, 2 * FACTOR_RANK)
    return (left, right)
```

```python
import functools
import math

import jax
import jax.numpy as jnp
import numpy as np
from jax import lax
from jax.experimental import pallas as pl
from jax.experimental.pallas import tpu as pltpu
from jax.sharding import PartitionSpec as P

ITERS = 2
MESH = pl.DeviceIdType.MESH
HIGHEST = lax.Precision.HIGHEST

complete_cycle = 2.0 * math.pi


def sine_coefficients(terms=8):
    nodes = np.cos(np.pi * (np.arange(400) + 0.5) / 400)
    r = 0.25 + 0.25 * nodes
    values = np.sin(2 * np.pi * r) / r
    square = r * r
    scaled = square * 8 - 1
    fit = np.polynomial.chebyshev.chebfit(scaled, values, terms - 1)
    series = np.polynomial.chebyshev.cheb2poly(fit)
    power = np.zeros(1)
    for c in series[::-1]:
        power = np.polynomial.polynomial.polyadd(
            np.polynomial.polynomial.polymul(power, [-1.0, 8.0]), [c]
        )
    return [float(c) for c in power[:terms]]


SINE = sine_coefficients()


def sine_of_cycles(x):
    r = x - jnp.round(x)
    s = r * r
    total = jnp.full_like(s, SINE[-1])
    for c in SINE[-2::-1]:
        total = total * s + c
    return total * r


def split(x):
    hi = x.astype(jnp.bfloat16)
    return hi, (x - hi.astype(jnp.float32)).astype(jnp.bfloat16)


def dot(a, b):
    return jnp.dot(a, b, preferred_element_type=jnp.float32)


def dot_nt(a, b, precision=None):
    return lax.dot_general(
        a, b, (((1,), (1,)), ((), ())), precision=precision, preferred_element_type=jnp.float32
    )


def inverse_factors(grams):
    k = grams[0].shape[0]
    sub = lax.broadcasted_iota(jnp.int32, (k, 2 * k), 0)
    lane = lax.broadcasted_iota(jnp.int32, (k, 2 * k), 1)
    start = []
    for gram in grams:
        eye = (sub[:, :k] == lane[:, :k]).astype(jnp.float32)
        start.append(jnp.concatenate([gram, eye], axis=1))

    def step(i, state):
        out = []
        for x in state:
            row = jnp.sum(jnp.where(sub == i, x, 0.0), axis=0, keepdims=True)
            column = jnp.sum(jnp.where(lane == i, x, 0.0), axis=1, keepdims=True)
            pivot = jnp.sum(jnp.where(lane[:1] == i, row, 0.0), axis=1, keepdims=True)
            factor = jnp.where(sub[:, :1] > i, column / pivot, 0.0)
            out.append(x - factor * row)
        return tuple(out)

    done = lax.fori_loop(0, k, step, tuple(start))
    result = []
    for x in done:
        pivots = jnp.sum(jnp.where(sub == lane, x, 0.0), axis=1, keepdims=True)
        result.append(x[:, k:] * lax.rsqrt(pivots))
    return result


def kernel(
    n, groups, root, hid, whi_h, wlo_h, scale, retain, signs, left, right,
    whi, wlo, own, got, part, sums, res, gsend, grecv, factors, frecv,
    wsem, osem, hsend, hrecv, fsend, frsem, psend, precv, gs, gr, ms, mr,
):
    me = lax.axis_index("seq")
    core = lax.axis_index("head")
    tok, kblk = own.shape
    cols = whi.shape[1]
    half = tok // 2
    pieces = 2
    chunk = half // pieces
    heads = cols // 256

    def peer(r):
        return lax.rem(me + r, n)

    barrier = pltpu.get_barrier_semaphore()
    for r in range(1, n):
        pl.semaphore_signal(barrier, inc=1, device_id={"seq": peer(r)}, device_id_type=MESH)
    pl.semaphore_signal(barrier, inc=1, device_id={"head": 1 - core}, device_id_type=MESH)

    load_own = pltpu.make_async_copy(
        hid.at[:, pl.ds(pl.multiple_of(me * kblk, 128), kblk)], own, osem
    )
    load_own.start()
    load_hi = pltpu.make_async_copy(whi_h, whi, wsem.at[0])
    load_lo = pltpu.make_async_copy(wlo_h, wlo, wsem.at[1])
    load_hi.start()
    load_lo.start()
    pl.semaphore_wait(barrier, n)

    def rows_of(which, q):
        return pl.ds(pl.multiple_of(which * half + q * chunk, chunk), chunk)

    def hidden_copy(q, r):
        p = lax.rem(me + r, n)
        return pltpu.make_async_remote_copy(
            src_ref=hid.at[rows_of(core, q), pl.ds(pl.multiple_of(p * kblk, 128), kblk)],
            dst_ref=got.at[n - r - 1, rows_of(core, q)],
            send_sem=hsend.at[q, r - 1],
            recv_sem=hrecv.at[q, n - r - 1],
            device_id={"seq": p},
            device_id_type=MESH,
        )

    def hidden_arrival(q, slot):
        return pltpu.make_async_remote_copy(
            src_ref=got.at[slot, rows_of(core, q)],
            dst_ref=got.at[slot, rows_of(core, q)],
            send_sem=hsend.at[q, slot],
            recv_sem=hrecv.at[q, slot],
            device_id={"seq": lax.rem(me + slot + 1, n)},
            device_id_type=MESH,
        )

    def forward_copy(q, slot, which):
        return pltpu.make_async_remote_copy(
            src_ref=got.at[slot, rows_of(which, q)],
            dst_ref=got.at[slot, rows_of(which, q)],
            send_sem=fsend.at[q, slot],
            recv_sem=frsem.at[q, slot],
            device_id={"head": 1 - core},
            device_id_type=MESH,
        )

    def part_copy(slot, which, q):
        r = slot + 1
        return pltpu.make_async_remote_copy(
            src_ref=part.at[slot, rows_of(which, q)],
            dst_ref=sums.at[n - r - 1, rows_of(which, q)],
            send_sem=psend.at[slot, which, q],
            recv_sem=precv.at[n - r - 1, which, q],
            device_id={"seq": lax.rem(me + r, n)},
            device_id_type=MESH,
        )

    def part_arrival(slot, which, q):
        return pltpu.make_async_remote_copy(
            src_ref=sums.at[slot, rows_of(which, q)],
            dst_ref=sums.at[slot, rows_of(which, q)],
            send_sem=psend.at[slot, which, q],
            recv_sem=precv.at[slot, which, q],
            device_id={"seq": lax.rem(me + slot + 1, n)},
            device_id_type=MESH,
        )

    for q in range(pieces):
        for r in range(1, n):
            hidden_copy(q, r).start()

    def project(src, dst, rows):
        hi, lo = split(src[rows])

        def tile(t, carry):
            c = pl.ds(pl.multiple_of(t * 256, 256), 256)
            w = whi[:, c]
            dst[rows, c] = dot(hi, w) + dot(lo, w) + dot(hi, wlo[:, c])
            return carry

        lax.fori_loop(0, cols // 256, tile, 0)

    load_own.wait()
    load_hi.wait()
    load_lo.wait()

    def own_step(i, carry):
        project(own, res, pl.ds(pl.multiple_of(i * chunk, chunk), chunk))
        return carry

    lax.fori_loop(0, tok // chunk, own_step, 0)

    def step(i, carry):
        q = i // (n - 1)
        slot = lax.rem(i, n - 1)
        hidden_arrival(q, slot).wait_recv()
        forward_copy(q, slot, core).start()

        def side(j, carry):
            which = lax.rem(core + j, 2)

            @pl.when(j == 1)
            def _():
                forward_copy(q, slot, which).wait_recv()

            project(got.at[slot], part.at[slot], rows_of(which, q))
            part_copy(slot, which, q).start()
            return carry

        lax.fori_loop(0, 2, side, 0)
        return carry

    lax.fori_loop(0, pieces * (n - 1), step, 0)

    group = tok // groups
    per = chunk // group

    def residual(i, carry):
        which = i // pieces
        q = lax.rem(i, pieces)
        for slot in range(n - 1):
            part_arrival(slot, which, q).wait_recv()
        for g in range(per):
            at = i * per + g
            rows = pl.ds(pl.multiple_of(at * group, group), group)
            kv = res[rows]
            for slot in range(n - 1):
                kv = kv + sums[slot, rows]
            kv = kv * scale[rows]
            spacing = jnp.max(jnp.abs(kv), axis=0, keepdims=True) / 7.0 + 1e-06
            res[rows] = retain[pl.ds(at, 1)] * sine_of_cycles(kv * (1.0 / spacing))
        return carry

    lax.fori_loop(0, 2 * pieces, residual, 0)

    def square(h, carry):
        for e in range(2):
            hi, lo = split(res[:, pl.ds(pl.multiple_of(h * 256 + e * 128, 128), 128)])
            both = jnp.concatenate([hi, lo], axis=1)
            g = lax.dot_general(
                both, both, (((0,), (0,)), ((), ())), preferred_element_type=jnp.float32
            )
            gsend[h, e] = g[:128, :128] + (g[:128, 128:] + g[128:, :128])
        return carry

    lax.fori_loop(0, heads, square, 0)

    def gram_copy(r):
        p = peer(r)
        return pltpu.make_async_remote_copy(
            src_ref=gsend.at[p],
            dst_ref=grecv.at[n - r - 1],
            send_sem=gs.at[r - 1],
            recv_sem=gr.at[n - r - 1],
            device_id={"seq": p},
            device_id_type=MESH,
        )

    for r in range(1, n):
        gram_copy(r).start()
    for r in range(1, n):
        gram_copy(r).wait_recv()

    total = [gsend[me, e] for e in range(2)]
    for slot in range(n - 1):
        total = [total[e] + grecv[slot, e] for e in range(2)]
    sketch = [signs[me, e] for e in range(2)]
    for iteration in range(ITERS):
        product = [jnp.dot(sketch[e], total[e], precision=HIGHEST) for e in range(2)]
        inverse = inverse_factors([dot_nt(product[e], sketch[e], HIGHEST) for e in range(2)])
        coefficient = [jnp.dot(inverse[e], product[e], precision=HIGHEST) for e in range(2)]
        if iteration + 1 < ITERS:
            sketch = coefficient
        else:
            sketch = [jnp.dot(inverse[e], sketch[e], precision=HIGHEST) for e in range(2)]
    rank = sketch[0].shape[0]
    for e in range(2):
        factors[0, e * rank : (e + 1) * rank] = sketch[e] * root
    factors[1] = jnp.concatenate(coefficient, axis=0).T * (1.0 / root)

    def factor_copy(r):
        return pltpu.make_async_remote_copy(
            src_ref=factors,
            dst_ref=frecv.at[n - r - 1],
            send_sem=ms.at[r - 1],
            recv_sem=mr.at[n - r - 1],
            device_id={"seq": peer(r)},
            device_id_type=MESH,
        )

    for r in range(1, n):
        factor_copy(r).start()

    def finish(h, matrix, coefficient_rows):
        zero = jnp.zeros((rank, 128), jnp.float32)
        block = jnp.concatenate(
            [
                jnp.concatenate([matrix[:rank], zero], axis=1),
                jnp.concatenate([zero, matrix[rank:]], axis=1),
            ],
            axis=0,
        )
        mhi, mlo = split(block)
        hi, lo = split(res[:, pl.ds(pl.multiple_of(h * 256, 256), 256)])
        value = dot_nt(hi, mhi) + (dot_nt(lo, mhi) + dot_nt(hi, mlo))
        left[h] = value.astype(jnp.bfloat16)
        right[h] = coefficient_rows

    finish(me, factors[0], factors[1])
    for r in range(1, n):
        slot = r - 1
        factor_copy(n - r).wait_recv()
        finish(peer(r), frecv[slot, 0], frecv[slot, 1])

    for q in range(pieces):
        for r in range(1, n):
            hidden_copy(q, r).wait_send()
            forward_copy(q, r - 1, core).wait_send()
            for which in range(2):
                part_copy(r - 1, which, q).wait_send()
    for r in range(1, n):
        gram_copy(r).wait_send()
        factor_copy(r).wait_send()


def fast_shards(n, hidden, row_scale, key_value_weight, outlier, sketch_sign_flags):
    tok = hidden.shape[0]
    kblk, heads, per_head = key_value_weight.shape
    cols = heads * per_head
    groups = outlier.shape[0]
    flat = key_value_weight.reshape(kblk, cols)
    top = lax.reduce_precision(flat, exponent_bits=8, mantissa_bits=7)
    whi = top.astype(jnp.bfloat16)
    wlo = (flat - top).astype(jnp.bfloat16)
    retain = jnp.repeat((1 - outlier).astype(jnp.float32), per_head, axis=1)
    signs = (2 * sketch_sign_flags - 1).astype(jnp.float32).transpose(0, 1, 3, 2)
    f32 = jnp.float32
    any_spec = pl.BlockSpec(memory_space=pl.ANY)
    vmem = pl.BlockSpec(memory_space=pltpu.VMEM)
    dma = pltpu.SemaphoreType.DMA
    left, right = pl.pallas_call(
        functools.partial(kernel, n, groups, math.sqrt(tok * n)),
        out_shape=(
            jax.ShapeDtypeStruct((heads, tok, 128), jnp.bfloat16),
            jax.ShapeDtypeStruct((heads, 128, 128), f32),
        ),
        in_specs=[any_spec, any_spec, any_spec, vmem, vmem, vmem],
        out_specs=(vmem, vmem),
        scratch_shapes=[
            pltpu.VMEM((kblk, cols), jnp.bfloat16),
            pltpu.VMEM((kblk, cols), jnp.bfloat16),
            pltpu.VMEM((tok, kblk), f32),
            pltpu.VMEM((n - 1, tok, kblk), f32),
            pltpu.VMEM((n - 1, tok, cols), f32),
            pltpu.VMEM((n - 1, tok, cols), f32),
            pltpu.VMEM((tok, cols), f32),
            pltpu.VMEM((heads, 2, 128, 128), f32),
            pltpu.VMEM((n - 1, 2, 128, 128), f32),
            pltpu.VMEM((2, 128, 128), f32),
            pltpu.VMEM((n - 1, 2, 128, 128), f32),
            dma((2,)),
            dma,
            dma((2, n - 1)),
            dma((2, n - 1)),
            dma((2, n - 1)),
            dma((2, n - 1)),
            dma((n - 1, 2, 2)),
            dma((n - 1, 2, 2)),
            dma((n - 1,)),
            dma((n - 1,)),
            dma((n - 1,)),
            dma((n - 1,)),
        ],
        compiler_params=pltpu.CompilerParams(
            collective_id=0, has_side_effects=True, vmem_limit_bytes=56 * 1024 * 1024
        ),
        cost_estimate=pl.CostEstimate(
            flops=6 * n * tok * kblk * cols, bytes_accessed=4 * n * tok * kblk, transcendentals=0
        ),
    )(hidden, whi, wlo, row_scale[:, None], retain, signs)
    return left, right


def shards(hidden, row_scale, key_value_weight, outlier, sketch_sign_flags):
    tok_rows = hidden.shape[0]
    head_count = key_value_weight.shape[1]
    kv_cols = key_value_weight.shape[2]
    head_dim = kv_cols // 2
    rank_cols = sketch_sign_flags.shape[3]
    group_count = outlier.shape[0]
    highest = lax.Precision.HIGHEST
    weight_piece = lax.all_gather(key_value_weight, "seq", axis=0, tiled=True)
    flat_piece = weight_piece.reshape(weight_piece.shape[0], head_count * kv_cols)
    projected_key_value = jnp.dot(hidden, flat_piece, precision=highest)
    projected_key_value = projected_key_value * row_scale[:, None]
    grouped_rows = projected_key_value.reshape(
        group_count, tok_rows // group_count, head_count, kv_cols
    )
    quantization_spacing = jnp.max(jnp.abs(grouped_rows), axis=1, keepdims=True) / 7.0 + 1e-06
    retain_mask = (1 - outlier).astype(jnp.float32)[:, None, :, None]
    residual_error = (
        retain_mask * jnp.sin(complete_cycle * grouped_rows / quantization_spacing)
    ).reshape(tok_rows, head_count, 2, head_dim)
    sign_matrix = (2 * sketch_sign_flags - 1).astype(jnp.float32)
    sketch = jnp.einsum("thec,heck->thek", residual_error, sign_matrix, precision=highest)
    for iteration in range(ITERS):
        local_gram = jnp.einsum("thek,theq->hekq", sketch, sketch, precision=highest)
        gram_matrix = lax.psum(local_gram, "seq")
        lower_factor = jnp.linalg.cholesky(gram_matrix)
        identity = jnp.broadcast_to(jnp.eye(rank_cols, dtype=gram_matrix.dtype), gram_matrix.shape)
        inverse_factor = jax.scipy.linalg.solve_triangular(lower_factor, identity, lower=True)
        basis_matrix = jnp.einsum("thek,heqk->theq", sketch, inverse_factor, precision=highest)
        local_coef = jnp.einsum("thec,theq->hecq", residual_error, basis_matrix, precision=highest)
        coefficient_rows = lax.psum(local_coef, "seq")
        if iteration + 1 < ITERS:
            sketch = jnp.einsum(
                "thec,hecq->theq", residual_error, coefficient_rows, precision=highest
            )
    root_length = math.sqrt(tok_rows * lax.axis_size("seq"))
    left = (
        (root_length * basis_matrix)
        .transpose(1, 0, 2, 3)
        .reshape(head_count, tok_rows, 2 * rank_cols)
        .astype(jnp.bfloat16)
    )
    right = (
        (coefficient_rows / root_length)
        .transpose(0, 2, 1, 3)
        .reshape(head_count, head_dim, 2 * rank_cols)
    )
    return (left, right)


def solution(mesh):
    def run(hidden, row_scale, key_value_weight, outlier, sketch_sign_flags):
        members = mesh.shape["seq"]
        heads = key_value_weight.shape[1] // mesh.shape["head"]
        fits = members == 4 and heads == members and mesh.shape["head"] == 2
        chosen = functools.partial(fast_shards, members) if fits else shards
        return mapped(chosen)(hidden, row_scale, key_value_weight, outlier, sketch_sign_flags)

    def mapped(chosen):
        return jax.shard_map(
            chosen,
            mesh=mesh,
            in_specs=(
                P(("batch", "seq"), None),
                P(("batch", "seq")),
                P("seq", "head", None),
                P(("batch", "seq"), "head"),
                P("head", None, None, None),
            ),
            out_specs=(P("head", ("batch", "seq"), None), P(("batch", "head"), None, None)),
            check_vma=False,
        )

    return run
```

```python
import functools
import math

import jax
import jax.numpy as jnp
import numpy as np
from jax import lax
from jax.experimental import pallas as pl
from jax.experimental.pallas import tpu as pltpu
from jax.sharding import PartitionSpec as P

ITERS = 2
BLOCK = 4
MESH = pl.DeviceIdType.MESH
HIGHEST = lax.Precision.HIGHEST

complete_cycle = 2.0 * math.pi


def sine_coefficients(terms=8):
    nodes = np.cos(np.pi * (np.arange(400) + 0.5) / 400)
    r = 0.25 + 0.25 * nodes
    values = np.sin(2 * np.pi * r) / r
    square = r * r
    scaled = square * 8 - 1
    fit = np.polynomial.chebyshev.chebfit(scaled, values, terms - 1)
    series = np.polynomial.chebyshev.cheb2poly(fit)
    power = np.zeros(1)
    for c in series[::-1]:
        power = np.polynomial.polynomial.polyadd(
            np.polynomial.polynomial.polymul(power, [-1.0, 8.0]), [c]
        )
    return [float(c) for c in power[:terms]]


SINE = sine_coefficients()


def sine_of_cycles(x):
    r = x - jnp.round(x)
    s = r * r
    total = jnp.full_like(s, SINE[-1])
    for c in SINE[-2::-1]:
        total = total * s + c
    return total * r


def split(x):
    hi = x.astype(jnp.bfloat16)
    return hi, (x - hi.astype(jnp.float32)).astype(jnp.bfloat16)


def dot(a, b):
    return jnp.dot(a, b, preferred_element_type=jnp.float32)


def dot_nt(a, b, precision=None):
    return lax.dot_general(
        a, b, (((1,), (1,)), ((), ())), precision=precision, preferred_element_type=jnp.float32
    )


def inverse_factors(grams):
    k = grams[0].shape[0]
    sub = lax.broadcasted_iota(jnp.int32, (k, 2 * k), 0)
    lane = lax.broadcasted_iota(jnp.int32, (k, 2 * k), 1)
    start = []
    for gram in grams:
        eye = (sub[:, :k] == lane[:, :k]).astype(jnp.float32)
        start.append(jnp.concatenate([gram, eye], axis=1))

    def step(i, state):
        at = i * BLOCK
        out = []
        for x in state:
            rows, columns = [], []
            for t in range(BLOCK):
                rows.append(jnp.sum(jnp.where(sub == at + t, x, 0.0), axis=0, keepdims=True))
                picked = jnp.sum(jnp.where(lane == at + t, x, 0.0), axis=1, keepdims=True)
                columns.append(jnp.broadcast_to(picked, x.shape))
            for t in range(BLOCK):
                entry = [
                    jnp.sum(jnp.where(sub == at + u, columns[t], 0.0), axis=0, keepdims=True)
                    for u in range(t, BLOCK)
                ]
                inverse = 1.0 / entry[0]
                factor = jnp.where(sub > at + t, columns[t] * inverse, 0.0)
                for u in range(t + 1, BLOCK):
                    columns[u] = columns[u] - factor * entry[u - t]
                    rows[u] = rows[u] - (entry[u - t] * inverse) * rows[t]
                x = x - factor * rows[t]
            out.append(x)
        return tuple(out)

    done = lax.fori_loop(0, k // BLOCK, step, tuple(start))
    result = []
    for x in done:
        pivots = jnp.sum(jnp.where(sub == lane, x, 0.0), axis=1, keepdims=True)
        result.append(x[:, k:] * lax.rsqrt(pivots))
    return result


def kernel(
    n, groups, root, hid, weight, scale, retain, signs, left, right,
    whi, wlo, stage, own, got, part, sums, res, gsend, grecv, factors, frecv,
    wsem, osem, hsend, hrecv, fsend, frsem, psend, precv, gs, gr, ms, mr,
):
    me = lax.axis_index("seq")
    core = lax.axis_index("head")
    tok, kblk = own.shape
    cols = whi.shape[1]
    half = tok // 2
    pieces = 2
    chunk = half // pieces
    heads = cols // 256

    across = {1: me + 1 - 2 * lax.rem(me, 2), 2: lax.rem(me + 2, n), 3: n - 1 - me}

    def peer(m):
        return across[m]

    barrier = pltpu.get_barrier_semaphore()
    for r in range(1, n):
        pl.semaphore_signal(barrier, inc=1, device_id={"seq": peer(r)}, device_id_type=MESH)
    pl.semaphore_signal(barrier, inc=1, device_id={"head": 1 - core}, device_id_type=MESH)

    load_own = pltpu.make_async_copy(
        hid.at[:, pl.ds(pl.multiple_of(me * kblk, 128), kblk)], own, osem
    )
    load_own.start()
    depth = stage.shape[1]
    loads = kblk // depth

    def load_weight(i):
        slot = lax.rem(i, 2)
        return pltpu.make_async_copy(
            weight.at[pl.ds(pl.multiple_of(i * depth, depth), depth)], stage.at[slot], wsem.at[slot]
        )

    load_weight(0).start()
    pl.semaphore_wait(barrier, n)

    def rows_of(which, q):
        return pl.ds(pl.multiple_of(which * half + q * chunk, chunk), chunk)

    def hidden_copy(q, m):
        p = peer(m)
        return pltpu.make_async_remote_copy(
            src_ref=hid.at[rows_of(core, q), pl.ds(pl.multiple_of(p * kblk, 128), kblk)],
            dst_ref=got.at[m - 1, rows_of(core, q)],
            send_sem=hsend.at[q, m - 1],
            recv_sem=hrecv.at[q, m - 1],
            device_id={"seq": p},
            device_id_type=MESH,
        )

    def hidden_arrival(q, m):
        return pltpu.make_async_remote_copy(
            src_ref=got.at[m - 1, rows_of(core, q)],
            dst_ref=got.at[m - 1, rows_of(core, q)],
            send_sem=hsend.at[q, m - 1],
            recv_sem=hrecv.at[q, m - 1],
            device_id={"seq": peer(m)},
            device_id_type=MESH,
        )

    def forward_copy(q, m, which):
        return pltpu.make_async_remote_copy(
            src_ref=got.at[m - 1, rows_of(which, q)],
            dst_ref=got.at[m - 1, rows_of(which, q)],
            send_sem=fsend.at[q, m - 1],
            recv_sem=frsem.at[q, m - 1],
            device_id={"head": 1 - core},
            device_id_type=MESH,
        )

    def via_copy(which, q):
        return pltpu.make_async_remote_copy(
            src_ref=part.at[2, rows_of(which, q)],
            dst_ref=sums.at[2, rows_of(which, q)],
            send_sem=psend.at[2, which, q],
            recv_sem=precv.at[2, which, q],
            device_id={"seq": which * across[1] + (1 - which) * across[2]},
            device_id_type=MESH,
        )

    def part_copy(slot, which, q):
        return pltpu.make_async_remote_copy(
            src_ref=part.at[slot, rows_of(which, q)],
            dst_ref=sums.at[slot, rows_of(which, q)],
            send_sem=psend.at[slot, which, q],
            recv_sem=precv.at[slot, which, q],
            device_id={"seq": (1 - slot) * across[1] + slot * across[2]},
            device_id_type=MESH,
        )

    for q in range(pieces):
        for m in (3, 1, 2):
            hidden_copy(q, m).start()

    def project(src, dst, rows):
        hi, lo = split(src[rows])

        def tile(t, carry):
            c = pl.ds(pl.multiple_of(t * 256, 256), 256)
            w = whi[:, c]
            dst[rows, c] = dot(hi, w) + dot(lo, w) + dot(hi, wlo[:, c])
            return carry

        lax.fori_loop(0, cols // 256, tile, 0)

    def split_weight(i, carry):
        @pl.when(i + 1 < loads)
        def _():
            load_weight(i + 1).start()

        load_weight(i).wait()
        rows = pl.ds(pl.multiple_of(i * depth, depth), depth)
        for h in range(heads):
            hi, lo = split(stage[lax.rem(i, 2), :, h, :])
            whi[rows, h * 256 : (h + 1) * 256] = hi
            wlo[rows, h * 256 : (h + 1) * 256] = lo
        return carry

    lax.fori_loop(0, loads, split_weight, 0)
    load_own.wait()

    def own_step(i, carry):
        project(own, res, pl.ds(pl.multiple_of(i * chunk, chunk), chunk))
        return carry

    lax.fori_loop(0, tok // chunk, own_step, 0)

    def pass_on(i):
        q = i // 2
        which = lax.rem(core + i, 2)
        rows = rows_of(which, q)
        via_copy(which, q).wait_recv()
        part[which, rows] = part[which, rows] + sums[2, rows]
        part_copy(which, which, q).start()

    def step(i, carry):
        q = i // 2
        which = lax.rem(core + i, 2)
        for m in (3, 1, 2):

            @pl.when(lax.rem(i, 2) == 0)
            def _():
                hidden_arrival(q, m).wait_recv()
                forward_copy(q, m, core).start()

            @pl.when(lax.rem(i, 2) == 1)
            def _():
                forward_copy(q, m, 1 - core).wait_recv()

            project(got.at[m - 1], part.at[m - 1], rows_of(which, q))
            if m == 3:
                via_copy(which, q).start()
        part_copy(1 - which, which, q).start()

        @pl.when(i > 0)
        def _():
            pass_on(i - 1)

        return carry

    lax.fori_loop(0, 2 * pieces, step, 0)
    pass_on(2 * pieces - 1)

    group = tok // groups
    per = chunk // group

    def residual(i, carry):
        which = i // pieces
        q = lax.rem(i, pieces)
        for slot in range(2):
            part_copy(slot, which, q).wait_recv()
        for g in range(per):
            at = i * per + g
            rows = pl.ds(pl.multiple_of(at * group, group), group)
            kv = res[rows]
            for slot in range(2):
                kv = kv + sums[slot, rows]
            kv = kv * scale[rows]
            spacing = jnp.max(jnp.abs(kv), axis=0, keepdims=True) / 7.0 + 1e-06
            res[rows] = retain[pl.ds(at, 1)] * sine_of_cycles(kv * (1.0 / spacing))
        return carry

    lax.fori_loop(0, 2 * pieces, residual, 0)

    def square(h, carry):
        for e in range(2):
            hi, lo = split(res[:, pl.ds(pl.multiple_of(h * 256 + e * 128, 128), 128)])
            both = jnp.concatenate([hi, lo], axis=1)
            g = lax.dot_general(
                both, both, (((0,), (0,)), ((), ())), preferred_element_type=jnp.float32
            )
            gsend[h, e] = g[:128, :128] + (g[:128, 128:] + g[128:, :128])
        return carry

    lax.fori_loop(0, heads, square, 0)

    def gram_copy(m):
        return pltpu.make_async_remote_copy(
            src_ref=gsend.at[peer(m)],
            dst_ref=grecv.at[m - 1],
            send_sem=gs.at[m - 1],
            recv_sem=gr.at[m - 1],
            device_id={"seq": peer(m)},
            device_id_type=MESH,
        )

    for m in (3, 1, 2):
        gram_copy(m).start()
    for m in range(1, n):
        gram_copy(m).wait_recv()

    total = [gsend[me, e] for e in range(2)]
    for slot in range(n - 1):
        total = [total[e] + grecv[slot, e] for e in range(2)]
    sketch = [signs[me, e] for e in range(2)]
    for iteration in range(ITERS):
        product = [jnp.dot(sketch[e], total[e], precision=HIGHEST) for e in range(2)]
        inverse = inverse_factors([dot_nt(product[e], sketch[e], HIGHEST) for e in range(2)])
        coefficient = [jnp.dot(inverse[e], product[e], precision=HIGHEST) for e in range(2)]
        if iteration + 1 < ITERS:
            sketch = coefficient
        else:
            sketch = [jnp.dot(inverse[e], sketch[e], precision=HIGHEST) for e in range(2)]
    rank = sketch[0].shape[0]
    for e in range(2):
        factors[0, e * rank : (e + 1) * rank] = sketch[e] * root
    factors[1] = jnp.concatenate(coefficient, axis=0).T * (1.0 / root)

    def factor_copy(m):
        return pltpu.make_async_remote_copy(
            src_ref=factors,
            dst_ref=frecv.at[m - 1],
            send_sem=ms.at[m - 1],
            recv_sem=mr.at[m - 1],
            device_id={"seq": peer(m)},
            device_id_type=MESH,
        )

    for m in (3, 1, 2):
        factor_copy(m).start()

    def finish(h, matrix, coefficient_rows):
        zero = jnp.zeros((rank, 128), jnp.float32)
        block = jnp.concatenate(
            [
                jnp.concatenate([matrix[:rank], zero], axis=1),
                jnp.concatenate([zero, matrix[rank:]], axis=1),
            ],
            axis=0,
        )
        mhi, mlo = split(block)
        hi, lo = split(res[:, pl.ds(pl.multiple_of(h * 256, 256), 256)])
        value = dot_nt(hi, mhi) + (dot_nt(lo, mhi) + dot_nt(hi, mlo))
        left[h] = value.astype(jnp.bfloat16)
        right[h] = coefficient_rows

    finish(me, factors[0], factors[1])
    for m in range(1, n):
        factor_copy(m).wait_recv()
        finish(peer(m), frecv[m - 1, 0], frecv[m - 1, 1])

    for q in range(pieces):
        for m in range(1, n):
            hidden_copy(q, m).wait_send()
            forward_copy(q, m, core).wait_send()
        for which in range(2):
            via_copy(which, q).wait_send()
            for slot in range(2):
                part_copy(slot, which, q).wait_send()
    for m in range(1, n):
        gram_copy(m).wait_send()
        factor_copy(m).wait_send()


def fast_shards(n, hidden, row_scale, key_value_weight, outlier, sketch_sign_flags):
    tok = hidden.shape[0]
    kblk, heads, per_head = key_value_weight.shape
    cols = heads * per_head
    groups = outlier.shape[0]
    retain = jnp.repeat((1 - outlier).astype(jnp.float32), per_head, axis=1)
    signs = (2 * sketch_sign_flags - 1).astype(jnp.float32).transpose(0, 1, 3, 2)
    f32 = jnp.float32
    any_spec = pl.BlockSpec(memory_space=pl.ANY)
    vmem = pl.BlockSpec(memory_space=pltpu.VMEM)
    dma = pltpu.SemaphoreType.DMA
    left, right = pl.pallas_call(
        functools.partial(kernel, n, groups, math.sqrt(tok * n)),
        out_shape=(
            jax.ShapeDtypeStruct((heads, tok, 128), jnp.bfloat16),
            jax.ShapeDtypeStruct((heads, 128, 128), f32),
        ),
        in_specs=[any_spec, any_spec, vmem, vmem, vmem],
        out_specs=(vmem, vmem),
        scratch_shapes=[
            pltpu.VMEM((kblk, cols), jnp.bfloat16),
            pltpu.VMEM((kblk, cols), jnp.bfloat16),
            pltpu.VMEM((2, math.gcd(kblk, 256), heads, per_head), f32),
            pltpu.VMEM((tok, kblk), f32),
            pltpu.VMEM((n - 1, tok, kblk), f32),
            pltpu.VMEM((n - 1, tok, cols), f32),
            pltpu.VMEM((n - 1, tok, cols), f32),
            pltpu.VMEM((tok, cols), f32),
            pltpu.VMEM((heads, 2, 128, 128), f32),
            pltpu.VMEM((n - 1, 2, 128, 128), f32),
            pltpu.VMEM((2, 128, 128), f32),
            pltpu.VMEM((n - 1, 2, 128, 128), f32),
            dma((2,)),
            dma,
            dma((2, n - 1)),
            dma((2, n - 1)),
            dma((2, n - 1)),
            dma((2, n - 1)),
            dma((n - 1, 2, 2)),
            dma((n - 1, 2, 2)),
            dma((n - 1,)),
            dma((n - 1,)),
            dma((n - 1,)),
            dma((n - 1,)),
        ],
        compiler_params=pltpu.CompilerParams(
            collective_id=0, has_side_effects=True, vmem_limit_bytes=56 * 1024 * 1024
        ),
        cost_estimate=pl.CostEstimate(
            flops=6 * n * tok * kblk * cols, bytes_accessed=4 * n * tok * kblk, transcendentals=0
        ),
    )(hidden, key_value_weight, row_scale[:, None], retain, signs)
    return left, right


def shards(hidden, row_scale, key_value_weight, outlier, sketch_sign_flags):
    tok_rows = hidden.shape[0]
    head_count = key_value_weight.shape[1]
    kv_cols = key_value_weight.shape[2]
    head_dim = kv_cols // 2
    rank_cols = sketch_sign_flags.shape[3]
    group_count = outlier.shape[0]
    highest = lax.Precision.HIGHEST
    weight_piece = lax.all_gather(key_value_weight, "seq", axis=0, tiled=True)
    flat_piece = weight_piece.reshape(weight_piece.shape[0], head_count * kv_cols)
    projected_key_value = jnp.dot(hidden, flat_piece, precision=highest)
    projected_key_value = projected_key_value * row_scale[:, None]
    grouped_rows = projected_key_value.reshape(
        group_count, tok_rows // group_count, head_count, kv_cols
    )
    quantization_spacing = jnp.max(jnp.abs(grouped_rows), axis=1, keepdims=True) / 7.0 + 1e-06
    retain_mask = (1 - outlier).astype(jnp.float32)[:, None, :, None]
    residual_error = (
        retain_mask * jnp.sin(complete_cycle * grouped_rows / quantization_spacing)
    ).reshape(tok_rows, head_count, 2, head_dim)
    sign_matrix = (2 * sketch_sign_flags - 1).astype(jnp.float32)
    sketch = jnp.einsum("thec,heck->thek", residual_error, sign_matrix, precision=highest)
    for iteration in range(ITERS):
        local_gram = jnp.einsum("thek,theq->hekq", sketch, sketch, precision=highest)
        gram_matrix = lax.psum(local_gram, "seq")
        lower_factor = jnp.linalg.cholesky(gram_matrix)
        identity = jnp.broadcast_to(jnp.eye(rank_cols, dtype=gram_matrix.dtype), gram_matrix.shape)
        inverse_factor = jax.scipy.linalg.solve_triangular(lower_factor, identity, lower=True)
        basis_matrix = jnp.einsum("thek,heqk->theq", sketch, inverse_factor, precision=highest)
        local_coef = jnp.einsum("thec,theq->hecq", residual_error, basis_matrix, precision=highest)
        coefficient_rows = lax.psum(local_coef, "seq")
        if iteration + 1 < ITERS:
            sketch = jnp.einsum(
                "thec,hecq->theq", residual_error, coefficient_rows, precision=highest
            )
    root_length = math.sqrt(tok_rows * lax.axis_size("seq"))
    left = (
        (root_length * basis_matrix)
        .transpose(1, 0, 2, 3)
        .reshape(head_count, tok_rows, 2 * rank_cols)
        .astype(jnp.bfloat16)
    )
    right = (
        (coefficient_rows / root_length)
        .transpose(0, 2, 1, 3)
        .reshape(head_count, head_dim, 2 * rank_cols)
    )
    return (left, right)


def solution(mesh):
    def run(hidden, row_scale, key_value_weight, outlier, sketch_sign_flags):
        members = mesh.shape["seq"]
        heads = key_value_weight.shape[1] // mesh.shape["head"]
        fits = members == 4 and heads == members and mesh.shape["head"] == 2
        chosen = functools.partial(fast_shards, members) if fits else shards
        return mapped(chosen)(hidden, row_scale, key_value_weight, outlier, sketch_sign_flags)

    def mapped(chosen):
        return jax.shard_map(
            chosen,
            mesh=mesh,
            in_specs=(
                P(("batch", "seq"), None),
                P(("batch", "seq")),
                P("seq", "head", None),
                P(("batch", "seq"), "head"),
                P("head", None, None, None),
            ),
            out_specs=(P("head", ("batch", "seq"), None), P(("batch", "head"), None, None)),
            check_vma=False,
        )

    return run
```

```python
import functools
import math

import jax
import jax.numpy as jnp
import numpy as np
from jax import lax
from jax.experimental import pallas as pl
from jax.experimental.pallas import tpu as pltpu
from jax.sharding import PartitionSpec as P

ITERS = 2
BLOCK = 4
PIECES = 2
AHEAD = 3
MESH = pl.DeviceIdType.MESH
HIGHEST = lax.Precision.HIGHEST

complete_cycle = 2.0 * math.pi


def sine_coefficients(terms=8):
    nodes = np.cos(np.pi * (np.arange(400) + 0.5) / 400)
    r = 0.25 + 0.25 * nodes
    values = np.sin(2 * np.pi * r) / r
    square = r * r
    scaled = square * 8 - 1
    fit = np.polynomial.chebyshev.chebfit(scaled, values, terms - 1)
    series = np.polynomial.chebyshev.cheb2poly(fit)
    power = np.zeros(1)
    for c in series[::-1]:
        power = np.polynomial.polynomial.polyadd(
            np.polynomial.polynomial.polymul(power, [-1.0, 8.0]), [c]
        )
    return [float(c) for c in power[:terms]]


SINE = sine_coefficients()


def sine_of_cycles(x):
    r = x - jnp.round(x)
    s = r * r
    total = jnp.full_like(s, SINE[-1])
    for c in SINE[-2::-1]:
        total = total * s + c
    return total * r


def split(x):
    hi = x.astype(jnp.bfloat16)
    return hi, (x - hi.astype(jnp.float32)).astype(jnp.bfloat16)


def dot(a, b):
    return jnp.dot(a, b, preferred_element_type=jnp.float32)


def dot_nt(a, b, precision=None):
    return lax.dot_general(
        a, b, (((1,), (1,)), ((), ())), precision=precision, preferred_element_type=jnp.float32
    )


def inverse_factors(grams):
    k = grams[0].shape[0]
    sub = lax.broadcasted_iota(jnp.int32, (k, 2 * k), 0)
    lane = lax.broadcasted_iota(jnp.int32, (k, 2 * k), 1)
    start = []
    for gram in grams:
        eye = (sub[:, :k] == lane[:, :k]).astype(jnp.float32)
        start.append(jnp.concatenate([gram, eye], axis=1))

    def step(i, state):
        at = i * BLOCK
        out = []
        for x in state:
            rows, columns = [], []
            for t in range(BLOCK):
                rows.append(jnp.sum(jnp.where(sub == at + t, x, 0.0), axis=0, keepdims=True))
                picked = jnp.sum(jnp.where(lane == at + t, x, 0.0), axis=1, keepdims=True)
                columns.append(jnp.broadcast_to(picked, x.shape))
            for t in range(BLOCK):
                entry = [
                    jnp.sum(jnp.where(sub == at + u, columns[t], 0.0), axis=0, keepdims=True)
                    for u in range(t, BLOCK)
                ]
                inverse = 1.0 / entry[0]
                factor = jnp.where(sub > at + t, columns[t] * inverse, 0.0)
                for u in range(t + 1, BLOCK):
                    columns[u] = columns[u] - factor * entry[u - t]
                    rows[u] = rows[u] - (entry[u - t] * inverse) * rows[t]
                x = x - factor * rows[t]
            out.append(x)
        return tuple(out)

    done = lax.fori_loop(0, k // BLOCK, step, tuple(start))
    result = []
    for x in done:
        pivots = jnp.sum(jnp.where(sub == lane, x, 0.0), axis=1, keepdims=True)
        result.append(x[:, k:] * lax.rsqrt(pivots))
    return result


def kernel(
    n, groups, root, hid, weight, scale, retain, signs, left, right, landed,
    whi, wlo, stage, own, got, part, sums, res, gsend, grecv, factors, frecv,
    lsem, osem, ysend, yrecv, zsend, zrecv, hsend, hrecv, fsend, frsem, psend, precv,
    gs, gr, ms, mr,
):
    me = lax.axis_index("seq")
    core = lax.axis_index("head")
    batch = lax.axis_index("batch")
    kblk = weight.shape[0]
    tok = own.shape[0]
    cols = whi.shape[1]
    half = tok // 2
    chunk = half // PIECES
    heads = cols // 256
    across = {1: me + 1 - 2 * lax.rem(me, 2), 2: lax.rem(me + 2, n), 3: n - 1 - me}
    parity = lax.rem(batch, 2)
    twin = batch + 1 - 2 * parity

    def peer(m):
        return across[m]

    barrier = pltpu.get_barrier_semaphore()
    for m in range(1, n):
        pl.semaphore_signal(barrier, inc=1, device_id={"seq": peer(m)}, device_id_type=MESH)
    pl.semaphore_signal(barrier, inc=1, device_id={"head": 1 - core}, device_id_type=MESH)
    pl.semaphore_signal(barrier, inc=1, device_id={"batch": twin}, device_id_type=MESH)

    def columns_of(member):
        return pl.ds(pl.multiple_of(member * kblk, 128), kblk)

    load_own = [
        pltpu.make_async_copy(
            hid.at[:, columns_of(p)], own.at[:, pl.ds(b * kblk, kblk)], osem.at[b]
        )
        for b, p in enumerate((me, across[2]))
    ]
    for copy in load_own:
        copy.start()
    depth = stage.shape[1]
    loads = kblk // depth

    def load_weight(source, i, slot):
        return pltpu.make_async_copy(
            source.at[pl.ds(pl.multiple_of(i * depth, depth), depth)], stage.at[slot], lsem.at[slot]
        )

    def split_stage(slot, at):
        rows = pl.ds(pl.multiple_of(at, depth), depth)
        for h in range(heads):
            hi, lo = split(stage[slot, :, h, :])
            whi[rows, h * 256 : (h + 1) * 256] = hi
            wlo[rows, h * 256 : (h + 1) * 256] = lo

    load_weight(weight, 0, 0).start()
    pl.semaphore_wait(barrier, n + 1)

    def rows_of(which, q):
        return pl.ds(pl.multiple_of(which * half + q * chunk, chunk), chunk)

    share = loads // 2

    def weight_rows(which, i):
        return pl.ds(pl.multiple_of((which * share + i) * depth, depth), depth)

    def weight_copy(i):
        return pltpu.make_async_remote_copy(
            src_ref=weight.at[weight_rows(parity, i)],
            dst_ref=landed.at[weight_rows(parity, i)],
            send_sem=ysend.at[i],
            recv_sem=yrecv.at[i],
            device_id={"seq": across[2]},
            device_id_type=MESH,
        )

    def twin_copy(i, which):
        return pltpu.make_async_remote_copy(
            src_ref=landed.at[weight_rows(which, i)],
            dst_ref=landed.at[weight_rows(which, i)],
            send_sem=zsend.at[i],
            recv_sem=zrecv.at[i],
            device_id={"batch": twin},
            device_id_type=MESH,
        )

    def hidden_copy(q, b):
        return pltpu.make_async_remote_copy(
            src_ref=hid.at[rows_of(core, q), columns_of((1 - b) * across[1] + b * across[3])],
            dst_ref=got.at[rows_of(core, q), columns_of(b)],
            send_sem=hsend.at[q, b],
            recv_sem=hrecv.at[q, b],
            device_id={"seq": across[1]},
            device_id_type=MESH,
        )

    def forward_copy(q, b, which):
        return pltpu.make_async_remote_copy(
            src_ref=got.at[rows_of(which, q), columns_of(b)],
            dst_ref=got.at[rows_of(which, q), columns_of(b)],
            send_sem=fsend.at[q, b],
            recv_sem=frsem.at[q, b],
            device_id={"head": 1 - core},
            device_id_type=MESH,
        )

    def part_copy(which, q):
        return pltpu.make_async_remote_copy(
            src_ref=part.at[rows_of(which, q)],
            dst_ref=sums.at[rows_of(which, q)],
            send_sem=psend.at[which, q],
            recv_sem=precv.at[which, q],
            device_id={"seq": across[1]},
            device_id_type=MESH,
        )

    def project(src, dst, rows, b, add):
        hi, lo = split(src[rows, b * kblk : (b + 1) * kblk])
        depths = slice(b * kblk, (b + 1) * kblk)

        def tile(t, carry):
            c = pl.ds(pl.multiple_of(t * 256, 256), 256)
            w = whi[depths, c]
            value = dot(hi, w) + dot(lo, w) + dot(hi, wlo[depths, c])
            dst[rows, c] = dst[rows, c] + value if add else value
            return carry

        lax.fori_loop(0, cols // 256, tile, 0)

    hidden_order = [(q, b) for q in range(PIECES) for b in range(2)]
    for i in range(AHEAD):
        weight_copy(i).start()
    for q, b in hidden_order[:2]:
        hidden_copy(q, b).start()

    def split_own(i, carry):
        slot = lax.rem(i, 2)

        @pl.when(i + 1 < loads)
        def _():
            load_weight(weight, i + 1, 1 - slot).start()

        load_weight(weight, i, slot).wait()
        split_stage(slot, i * depth)
        return carry

    lax.fori_loop(0, loads, split_own, 0)
    for copy in load_own:
        copy.wait()

    def own_first(i, carry):
        project(own, res, pl.ds(pl.multiple_of(i * chunk, chunk), chunk), 0, False)
        return carry

    lax.fori_loop(0, 2 * PIECES, own_first, 0)

    every = share // len(hidden_order)

    def arrive(i, carry):
        weight_copy(i).wait_recv()
        twin_copy(i, parity).start()

        @pl.when(i + AHEAD < share)
        def _():
            weight_copy(i + AHEAD).start()

        direct = load_weight(landed, parity * share + i, 0)
        direct.start()

        @pl.when(lax.rem(i, every) == every - 1)
        def _():
            at = i // every
            hidden_copy(at // 2, lax.rem(at, 2)).wait_recv()
            forward_copy(at // 2, lax.rem(at, 2), core).start()

            @pl.when(at + 2 < len(hidden_order))
            def _():
                hidden_copy(at // 2 + 1, lax.rem(at, 2)).start()

        def passed():
            return load_weight(landed, (1 - parity) * share + i - 1, 1)

        @pl.when(i > 0)
        def _():
            twin_copy(i - 1, 1 - parity).wait_recv()
            passed().start()

        direct.wait()
        split_stage(0, kblk + (parity * share + i) * depth)

        @pl.when(i > 0)
        def _():
            passed().wait()
            split_stage(1, kblk + ((1 - parity) * share + i - 1) * depth)

        return carry

    lax.fori_loop(0, share, arrive, 0)
    twin_copy(share - 1, 1 - parity).wait_recv()
    passed = load_weight(landed, (1 - parity) * share + share - 1, 1)
    passed.start()
    passed.wait()
    split_stage(1, kblk + ((1 - parity) * share + share - 1) * depth)

    def neighbour(i, carry):
        q = i // 2
        which = lax.rem(core + i, 2)

        @pl.when(lax.rem(i, 2) == 1)
        def _():
            for b in range(2):
                forward_copy(q, b, which).wait_recv()

        rows = rows_of(which, q)
        project(got, part, rows, 0, False)
        project(got, part, rows, 1, True)
        part_copy(which, q).start()
        return carry

    lax.fori_loop(0, 2 * PIECES, neighbour, 0)

    def own_step(i, carry):
        project(own, res, pl.ds(pl.multiple_of(i * chunk, chunk), chunk), 1, True)
        return carry

    lax.fori_loop(0, 2 * PIECES, own_step, 0)

    group = tok // groups
    per = chunk // group

    def residual(i, carry):
        q = i // 2
        which = lax.rem(core + i, 2)
        part_copy(which, q).wait_recv()
        for g in range(per):
            at = (which * PIECES + q) * per + g
            rows = pl.ds(pl.multiple_of(at * group, group), group)
            kv = (res[rows] + sums[rows]) * scale[rows]
            spacing = jnp.max(jnp.abs(kv), axis=0, keepdims=True) / 7.0 + 1e-06
            res[rows] = retain[pl.ds(at, 1)] * sine_of_cycles(kv * (1.0 / spacing))
        return carry

    lax.fori_loop(0, 2 * PIECES, residual, 0)

    def square(h, carry):
        for e in range(2):
            hi, lo = split(res[:, pl.ds(pl.multiple_of(h * 256 + e * 128, 128), 128)])
            both = jnp.concatenate([hi, lo], axis=1)
            g = lax.dot_general(
                both, both, (((0,), (0,)), ((), ())), preferred_element_type=jnp.float32
            )
            gsend[h, e] = g[:128, :128] + (g[:128, 128:] + g[128:, :128])
        return carry

    lax.fori_loop(0, heads, square, 0)

    def gram_copy(m):
        return pltpu.make_async_remote_copy(
            src_ref=gsend.at[peer(m)],
            dst_ref=grecv.at[m - 1],
            send_sem=gs.at[m - 1],
            recv_sem=gr.at[m - 1],
            device_id={"seq": peer(m)},
            device_id_type=MESH,
        )

    for m in (3, 1, 2):
        gram_copy(m).start()
    for m in range(1, n):
        gram_copy(m).wait_recv()

    total = [gsend[me, e] for e in range(2)]
    for slot in range(n - 1):
        total = [total[e] + grecv[slot, e] for e in range(2)]
    sketch = [signs[me, e] for e in range(2)]
    for iteration in range(ITERS):
        product = [jnp.dot(sketch[e], total[e], precision=HIGHEST) for e in range(2)]
        inverse = inverse_factors([dot_nt(product[e], sketch[e], HIGHEST) for e in range(2)])
        coefficient = [jnp.dot(inverse[e], product[e], precision=HIGHEST) for e in range(2)]
        if iteration + 1 < ITERS:
            sketch = coefficient
        else:
            sketch = [jnp.dot(inverse[e], sketch[e], precision=HIGHEST) for e in range(2)]
    rank = sketch[0].shape[0]
    for e in range(2):
        factors[0, e * rank : (e + 1) * rank] = sketch[e] * root
    factors[1] = jnp.concatenate(coefficient, axis=0).T * (1.0 / root)

    def factor_copy(m):
        return pltpu.make_async_remote_copy(
            src_ref=factors,
            dst_ref=frecv.at[m - 1],
            send_sem=ms.at[m - 1],
            recv_sem=mr.at[m - 1],
            device_id={"seq": peer(m)},
            device_id_type=MESH,
        )

    for m in (3, 1, 2):
        factor_copy(m).start()

    def finish(h, matrix, coefficient_rows):
        zero = jnp.zeros((rank, 128), jnp.float32)
        block = jnp.concatenate(
            [
                jnp.concatenate([matrix[:rank], zero], axis=1),
                jnp.concatenate([zero, matrix[rank:]], axis=1),
            ],
            axis=0,
        )
        mhi, mlo = split(block)
        hi, lo = split(res[:, pl.ds(pl.multiple_of(h * 256, 256), 256)])
        value = dot_nt(hi, mhi) + (dot_nt(lo, mhi) + dot_nt(hi, mlo))
        left[h] = value.astype(jnp.bfloat16)
        right[h] = coefficient_rows

    finish(me, factors[0], factors[1])
    for m in range(1, n):
        factor_copy(m).wait_recv()
        finish(peer(m), frecv[m - 1, 0], frecv[m - 1, 1])

    for i in range(share):
        weight_copy(i).wait_send()
        twin_copy(i, parity).wait_send()
    for q in range(PIECES):
        for b in range(2):
            hidden_copy(q, b).wait_send()
            forward_copy(q, b, core).wait_send()
            part_copy(b, q).wait_send()
    for m in range(1, n):
        gram_copy(m).wait_send()
        factor_copy(m).wait_send()


def fast_shards(n, hidden, row_scale, key_value_weight, outlier, sketch_sign_flags):
    tok = hidden.shape[0]
    kblk, heads, per_head = key_value_weight.shape
    cols = heads * per_head
    groups = outlier.shape[0]
    retain = jnp.repeat((1 - outlier).astype(jnp.float32), per_head, axis=1)
    signs = (2 * sketch_sign_flags - 1).astype(jnp.float32).transpose(0, 1, 3, 2)
    f32 = jnp.float32
    any_spec = pl.BlockSpec(memory_space=pl.ANY)
    vmem = pl.BlockSpec(memory_space=pltpu.VMEM)
    dma = pltpu.SemaphoreType.DMA
    depth = kblk // 16
    left, right, _ = pl.pallas_call(
        functools.partial(kernel, n, groups, math.sqrt(tok * n)),
        out_shape=(
            jax.ShapeDtypeStruct((heads, tok, 128), jnp.bfloat16),
            jax.ShapeDtypeStruct((heads, 128, 128), f32),
            jax.ShapeDtypeStruct((kblk, heads, per_head), f32),
        ),
        in_specs=[any_spec, any_spec, vmem, vmem, vmem],
        out_specs=(vmem, vmem, any_spec),
        scratch_shapes=[
            pltpu.VMEM((2 * kblk, cols), jnp.bfloat16),
            pltpu.VMEM((2 * kblk, cols), jnp.bfloat16),
            pltpu.VMEM((2, depth, heads, per_head), f32),
            pltpu.VMEM((tok, 2 * kblk), f32),
            pltpu.VMEM((tok, 2 * kblk), f32),
            pltpu.VMEM((tok, cols), f32),
            pltpu.VMEM((tok, cols), f32),
            pltpu.VMEM((tok, cols), f32),
            pltpu.VMEM((heads, 2, 128, 128), f32),
            pltpu.VMEM((n - 1, 2, 128, 128), f32),
            pltpu.VMEM((2, 128, 128), f32),
            pltpu.VMEM((n - 1, 2, 128, 128), f32),
            dma((2,)),
            dma((2,)),
            dma((8,)),
            dma((8,)),
            dma((8,)),
            dma((8,)),
            dma((PIECES, 2)),
            dma((PIECES, 2)),
            dma((PIECES, 2)),
            dma((PIECES, 2)),
            dma((2, PIECES)),
            dma((2, PIECES)),
            dma((n - 1,)),
            dma((n - 1,)),
            dma((n - 1,)),
            dma((n - 1,)),
        ],
        compiler_params=pltpu.CompilerParams(
            collective_id=0, has_side_effects=True, vmem_limit_bytes=56 * 1024 * 1024
        ),
        cost_estimate=pl.CostEstimate(
            flops=6 * n * tok * kblk * cols, bytes_accessed=4 * n * tok * kblk, transcendentals=0
        ),
    )(hidden, key_value_weight, row_scale[:, None], retain, signs)
    return left, right


def shards(hidden, row_scale, key_value_weight, outlier, sketch_sign_flags):
    tok_rows = hidden.shape[0]
    head_count = key_value_weight.shape[1]
    kv_cols = key_value_weight.shape[2]
    head_dim = kv_cols // 2
    rank_cols = sketch_sign_flags.shape[3]
    group_count = outlier.shape[0]
    highest = lax.Precision.HIGHEST
    weight_piece = lax.all_gather(key_value_weight, "seq", axis=0, tiled=True)
    flat_piece = weight_piece.reshape(weight_piece.shape[0], head_count * kv_cols)
    projected_key_value = jnp.dot(hidden, flat_piece, precision=highest)
    projected_key_value = projected_key_value * row_scale[:, None]
    grouped_rows = projected_key_value.reshape(
        group_count, tok_rows // group_count, head_count, kv_cols
    )
    quantization_spacing = jnp.max(jnp.abs(grouped_rows), axis=1, keepdims=True) / 7.0 + 1e-06
    retain_mask = (1 - outlier).astype(jnp.float32)[:, None, :, None]
    residual_error = (
        retain_mask * jnp.sin(complete_cycle * grouped_rows / quantization_spacing)
    ).reshape(tok_rows, head_count, 2, head_dim)
    sign_matrix = (2 * sketch_sign_flags - 1).astype(jnp.float32)
    sketch = jnp.einsum("thec,heck->thek", residual_error, sign_matrix, precision=highest)
    for iteration in range(ITERS):
        local_gram = jnp.einsum("thek,theq->hekq", sketch, sketch, precision=highest)
        gram_matrix = lax.psum(local_gram, "seq")
        lower_factor = jnp.linalg.cholesky(gram_matrix)
        identity = jnp.broadcast_to(jnp.eye(rank_cols, dtype=gram_matrix.dtype), gram_matrix.shape)
        inverse_factor = jax.scipy.linalg.solve_triangular(lower_factor, identity, lower=True)
        basis_matrix = jnp.einsum("thek,heqk->theq", sketch, inverse_factor, precision=highest)
        local_coef = jnp.einsum("thec,theq->hecq", residual_error, basis_matrix, precision=highest)
        coefficient_rows = lax.psum(local_coef, "seq")
        if iteration + 1 < ITERS:
            sketch = jnp.einsum(
                "thec,hecq->theq", residual_error, coefficient_rows, precision=highest
            )
    root_length = math.sqrt(tok_rows * lax.axis_size("seq"))
    left = (
        (root_length * basis_matrix)
        .transpose(1, 0, 2, 3)
        .reshape(head_count, tok_rows, 2 * rank_cols)
        .astype(jnp.bfloat16)
    )
    right = (
        (coefficient_rows / root_length)
        .transpose(0, 2, 1, 3)
        .reshape(head_count, head_dim, 2 * rank_cols)
    )
    return (left, right)


def solution(mesh):
    def run(hidden, row_scale, key_value_weight, outlier, sketch_sign_flags):
        members = mesh.shape["seq"]
        heads = key_value_weight.shape[1] // mesh.shape["head"]
        fits = members == 4 and heads == members
        fits = fits and mesh.shape["head"] == 2 and mesh.shape["batch"] % 2 == 0
        chosen = functools.partial(fast_shards, members) if fits else shards
        return mapped(chosen)(hidden, row_scale, key_value_weight, outlier, sketch_sign_flags)

    def mapped(chosen):
        return jax.shard_map(
            chosen,
            mesh=mesh,
            in_specs=(
                P(("batch", "seq"), None),
                P(("batch", "seq")),
                P("seq", "head", None),
                P(("batch", "seq"), "head"),
                P("head", None, None, None),
            ),
            out_specs=(P("head", ("batch", "seq"), None), P(("batch", "head"), None, None)),
            check_vma=False,
        )

    return run
```

```python
import functools
import math

import jax
import jax.numpy as jnp
import numpy as np
from jax import lax
from jax.experimental import pallas as pl
from jax.experimental.pallas import tpu as pltpu
from jax.sharding import PartitionSpec as P

ITERS = 2
BLOCK = 4
PIECES = 2
AHEAD = 4
MESH = pl.DeviceIdType.MESH
HIGHEST = lax.Precision.HIGHEST

complete_cycle = 2.0 * math.pi


def sine_coefficients(terms=8):
    nodes = np.cos(np.pi * (np.arange(400) + 0.5) / 400)
    r = 0.25 + 0.25 * nodes
    values = np.sin(2 * np.pi * r) / r
    square = r * r
    scaled = square * 8 - 1
    fit = np.polynomial.chebyshev.chebfit(scaled, values, terms - 1)
    series = np.polynomial.chebyshev.cheb2poly(fit)
    power = np.zeros(1)
    for c in series[::-1]:
        power = np.polynomial.polynomial.polyadd(
            np.polynomial.polynomial.polymul(power, [-1.0, 8.0]), [c]
        )
    return [float(c) for c in power[:terms]]


SINE = sine_coefficients()


def sine_of_cycles(x):
    r = x - jnp.round(x)
    s = r * r
    total = jnp.full_like(s, SINE[-1])
    for c in SINE[-2::-1]:
        total = total * s + c
    return total * r


def split(x):
    hi = x.astype(jnp.bfloat16)
    return hi, (x - hi.astype(jnp.float32)).astype(jnp.bfloat16)


def dot(a, b):
    return jnp.dot(a, b, preferred_element_type=jnp.float32)


def dot_nt(a, b, precision=None):
    return lax.dot_general(
        a, b, (((1,), (1,)), ((), ())), precision=precision, preferred_element_type=jnp.float32
    )


def inverse_factors(grams):
    k = grams[0].shape[0]
    sub = lax.broadcasted_iota(jnp.int32, (k, 2 * k), 0)
    lane = lax.broadcasted_iota(jnp.int32, (k, 2 * k), 1)
    start = []
    for gram in grams:
        eye = (sub[:, :k] == lane[:, :k]).astype(jnp.float32)
        start.append(jnp.concatenate([gram, eye], axis=1))

    def step(i, state):
        at = i * BLOCK
        out = []
        for x in state:
            rows, columns = [], []
            for t in range(BLOCK):
                rows.append(jnp.sum(jnp.where(sub == at + t, x, 0.0), axis=0, keepdims=True))
                picked = jnp.sum(jnp.where(lane == at + t, x, 0.0), axis=1, keepdims=True)
                columns.append(jnp.broadcast_to(picked, x.shape))
            for t in range(BLOCK):
                entry = [
                    jnp.sum(jnp.where(sub == at + u, columns[t], 0.0), axis=0, keepdims=True)
                    for u in range(t, BLOCK)
                ]
                inverse = 1.0 / entry[0]
                factor = jnp.where(sub > at + t, columns[t] * inverse, 0.0)
                for u in range(t + 1, BLOCK):
                    columns[u] = columns[u] - factor * entry[u - t]
                    rows[u] = rows[u] - (entry[u - t] * inverse) * rows[t]
                x = x - factor * rows[t]
            out.append(x)
        return tuple(out)

    done = lax.fori_loop(0, k // BLOCK, step, tuple(start))
    result = []
    for x in done:
        pivots = jnp.sum(jnp.where(sub == lane, x, 0.0), axis=1, keepdims=True)
        result.append(x[:, k:] * lax.rsqrt(pivots))
    return result


def kernel(
    n, groups, root, hid, weight, scale, retain, signs, left, right, landed,
    whi, wlo, stage, own, got, part, sums, res, gsend, grecv, factors, frecv,
    lsem, osem, ysend, yrecv, zsend, zrecv, hsend, hrecv, fsend, frsem, psend, precv,
    gs, gr, ms, mr,
):
    me = lax.axis_index("seq")
    core = lax.axis_index("head")
    batch = lax.axis_index("batch")
    kblk = weight.shape[0]
    tok = own.shape[0]
    cols = whi.shape[1]
    half = tok // 2
    chunk = half // PIECES
    heads = cols // 256
    across = {1: me + 1 - 2 * lax.rem(me, 2), 2: lax.rem(me + 2, n), 3: n - 1 - me}
    parity = lax.rem(batch, 2)
    twin = batch + 1 - 2 * parity

    def peer(m):
        return across[m]

    barrier = pltpu.get_barrier_semaphore()
    for m in range(1, n):
        pl.semaphore_signal(barrier, inc=1, device_id={"seq": peer(m)}, device_id_type=MESH)
    pl.semaphore_signal(barrier, inc=1, device_id={"head": 1 - core}, device_id_type=MESH)
    pl.semaphore_signal(barrier, inc=1, device_id={"batch": twin}, device_id_type=MESH)

    def columns_of(member):
        return pl.ds(pl.multiple_of(member * kblk, 128), kblk)

    load_own = [
        pltpu.make_async_copy(
            hid.at[:, columns_of(p)], own.at[:, pl.ds(b * kblk, kblk)], osem.at[b]
        )
        for b, p in enumerate((me, across[2]))
    ]
    for copy in load_own:
        copy.start()
    depth = stage.shape[1]
    loads = kblk // depth

    def load_weight(source, i, slot):
        return pltpu.make_async_copy(
            source.at[pl.ds(pl.multiple_of(i * depth, depth), depth)], stage.at[slot], lsem.at[slot]
        )

    def split_stage(slot, at):
        rows = pl.ds(pl.multiple_of(at, depth), depth)
        for h in range(heads):
            hi, lo = split(stage[slot, :, h, :])
            whi[rows, h * 256 : (h + 1) * 256] = hi
            wlo[rows, h * 256 : (h + 1) * 256] = lo

    load_weight(weight, 0, 0).start()
    pl.semaphore_wait(barrier, n + 1)

    def rows_of(which, q):
        return pl.ds(pl.multiple_of(which * half + q * chunk, chunk), chunk)

    share = loads // 2

    def weight_rows(which, i):
        return pl.ds(pl.multiple_of((which * share + i) * depth, depth), depth)

    def weight_copy(i):
        return pltpu.make_async_remote_copy(
            src_ref=weight.at[weight_rows(parity, i)],
            dst_ref=landed.at[weight_rows(parity, i)],
            send_sem=ysend.at[i],
            recv_sem=yrecv.at[i],
            device_id={"seq": across[2]},
            device_id_type=MESH,
        )

    def twin_copy(i, which):
        return pltpu.make_async_remote_copy(
            src_ref=landed.at[weight_rows(which, i)],
            dst_ref=landed.at[weight_rows(which, i)],
            send_sem=zsend.at[i],
            recv_sem=zrecv.at[i],
            device_id={"batch": twin},
            device_id_type=MESH,
        )

    def hidden_copy(q, b):
        return pltpu.make_async_remote_copy(
            src_ref=hid.at[rows_of(core, q), columns_of((1 - b) * across[1] + b * across[3])],
            dst_ref=got.at[rows_of(core, q), columns_of(b)],
            send_sem=hsend.at[q, b],
            recv_sem=hrecv.at[q, b],
            device_id={"seq": across[1]},
            device_id_type=MESH,
        )

    def forward_copy(q, b, which):
        return pltpu.make_async_remote_copy(
            src_ref=got.at[rows_of(which, q), columns_of(b)],
            dst_ref=got.at[rows_of(which, q), columns_of(b)],
            send_sem=fsend.at[q, b],
            recv_sem=frsem.at[q, b],
            device_id={"head": 1 - core},
            device_id_type=MESH,
        )

    def part_copy(which, q):
        return pltpu.make_async_remote_copy(
            src_ref=part.at[rows_of(which, q)],
            dst_ref=sums.at[rows_of(which, q)],
            send_sem=psend.at[which, q],
            recv_sem=precv.at[which, q],
            device_id={"seq": across[1]},
            device_id_type=MESH,
        )

    def project(src, dst, rows, b, add):
        hi, lo = split(src[rows, b * kblk : (b + 1) * kblk])
        depths = slice(b * kblk, (b + 1) * kblk)

        def tile(t, carry):
            c = pl.ds(pl.multiple_of(t * 256, 256), 256)
            w = whi[depths, c]
            value = dot(hi, w) + dot(lo, w) + dot(hi, wlo[depths, c])
            dst[rows, c] = dst[rows, c] + value if add else value
            return carry

        lax.fori_loop(0, cols // 256, tile, 0)

    hidden_order = [(q, b) for q in range(PIECES) for b in range(2)]
    for i in range(AHEAD):
        weight_copy(i).start()
    for q, b in hidden_order:
        hidden_copy(q, b).start()

    def split_own(i, carry):
        slot = lax.rem(i, 2)

        @pl.when(i + 1 < loads)
        def _():
            load_weight(weight, i + 1, 1 - slot).start()

        load_weight(weight, i, slot).wait()
        split_stage(slot, i * depth)
        return carry

    lax.fori_loop(0, loads, split_own, 0)
    for copy in load_own:
        copy.wait()

    def own_first(i, carry):
        project(own, res, pl.ds(pl.multiple_of(i * chunk, chunk), chunk), 0, False)
        return carry

    lax.fori_loop(0, 2 * PIECES, own_first, 0)


    def arrive(i, carry):
        weight_copy(i).wait_recv()
        twin_copy(i, parity).start()

        @pl.when(i + AHEAD < share)
        def _():
            weight_copy(i + AHEAD).start()

        direct = load_weight(landed, parity * share + i, 0)
        direct.start()

        def passed():
            return load_weight(landed, (1 - parity) * share + i - 1, 1)

        @pl.when(i > 0)
        def _():
            twin_copy(i - 1, 1 - parity).wait_recv()
            passed().start()

        direct.wait()
        split_stage(0, kblk + (parity * share + i) * depth)

        @pl.when(i > 0)
        def _():
            passed().wait()
            split_stage(1, kblk + ((1 - parity) * share + i - 1) * depth)

        return carry

    lax.fori_loop(0, share, arrive, 0)
    twin_copy(share - 1, 1 - parity).wait_recv()
    passed = load_weight(landed, (1 - parity) * share + share - 1, 1)
    passed.start()
    passed.wait()
    split_stage(1, kblk + ((1 - parity) * share + share - 1) * depth)

    for q, b in hidden_order:
        hidden_copy(q, b).wait_recv()
        forward_copy(q, b, core).start()

    def turn(i):
        return lax.rem(i, PIECES), lax.rem(core + i // PIECES, 2)

    def neighbour(i, carry):
        q, which = turn(i)

        @pl.when(i >= PIECES)
        def _():
            for b in range(2):
                forward_copy(q, b, which).wait_recv()

        rows = rows_of(which, q)
        project(got, part, rows, 0, False)
        project(got, part, rows, 1, True)
        part_copy(which, q).start()
        return carry

    lax.fori_loop(0, 2 * PIECES, neighbour, 0)

    def own_step(i, carry):
        project(own, res, pl.ds(pl.multiple_of(i * chunk, chunk), chunk), 1, True)
        return carry

    lax.fori_loop(0, 2 * PIECES, own_step, 0)

    group = tok // groups
    per = chunk // group

    def residual(i, carry):
        q, which = turn(i)
        part_copy(which, q).wait_recv()
        for g in range(per):
            at = (which * PIECES + q) * per + g
            rows = pl.ds(pl.multiple_of(at * group, group), group)
            kv = (res[rows] + sums[rows]) * scale[rows]
            spacing = jnp.max(jnp.abs(kv), axis=0, keepdims=True) / 7.0 + 1e-06
            res[rows] = retain[pl.ds(at, 1)] * sine_of_cycles(kv * (1.0 / spacing))
        rows = rows_of(which, q)

        def square(h, carry):
            for e in range(2):
                hi, lo = split(res[rows, pl.ds(pl.multiple_of(h * 256 + e * 128, 128), 128)])
                both = jnp.concatenate([hi, lo], axis=1)
                g = lax.dot_general(
                    both, both, (((0,), (0,)), ((), ())), preferred_element_type=jnp.float32
                )
                gsend[h, e] += g[:128, :128] + (g[:128, 128:] + g[128:, :128])
            return carry

        return lax.fori_loop(0, heads, square, carry)

    gsend[...] = jnp.zeros_like(gsend)
    lax.fori_loop(0, 2 * PIECES, residual, 0)

    def gram_copy(m):
        return pltpu.make_async_remote_copy(
            src_ref=gsend.at[peer(m)],
            dst_ref=grecv.at[m - 1],
            send_sem=gs.at[m - 1],
            recv_sem=gr.at[m - 1],
            device_id={"seq": peer(m)},
            device_id_type=MESH,
        )

    for m in (3, 1, 2):
        gram_copy(m).start()
    for m in range(1, n):
        gram_copy(m).wait_recv()

    total = [gsend[me, e] for e in range(2)]
    for slot in range(n - 1):
        total = [total[e] + grecv[slot, e] for e in range(2)]
    sketch = [signs[me, e] for e in range(2)]
    for iteration in range(ITERS):
        product = [jnp.dot(sketch[e], total[e], precision=HIGHEST) for e in range(2)]
        inverse = inverse_factors([dot_nt(product[e], sketch[e], HIGHEST) for e in range(2)])
        coefficient = [jnp.dot(inverse[e], product[e], precision=HIGHEST) for e in range(2)]
        if iteration + 1 < ITERS:
            sketch = coefficient
        else:
            sketch = [jnp.dot(inverse[e], sketch[e], precision=HIGHEST) for e in range(2)]
    rank = sketch[0].shape[0]
    for e in range(2):
        factors[0, e * rank : (e + 1) * rank] = sketch[e] * root
    factors[1] = jnp.concatenate(coefficient, axis=0).T * (1.0 / root)

    def factor_copy(m):
        return pltpu.make_async_remote_copy(
            src_ref=factors,
            dst_ref=frecv.at[m - 1],
            send_sem=ms.at[m - 1],
            recv_sem=mr.at[m - 1],
            device_id={"seq": peer(m)},
            device_id_type=MESH,
        )

    for m in (3, 1, 2):
        factor_copy(m).start()

    def finish(h, matrix, coefficient_rows):
        zero = jnp.zeros((rank, 128), jnp.float32)
        block = jnp.concatenate(
            [
                jnp.concatenate([matrix[:rank], zero], axis=1),
                jnp.concatenate([zero, matrix[rank:]], axis=1),
            ],
            axis=0,
        )
        mhi, mlo = split(block)
        hi, lo = split(res[:, pl.ds(pl.multiple_of(h * 256, 256), 256)])
        value = dot_nt(hi, mhi) + (dot_nt(lo, mhi) + dot_nt(hi, mlo))
        left[h] = value.astype(jnp.bfloat16)
        right[h] = coefficient_rows

    finish(me, factors[0], factors[1])
    for m in range(1, n):
        factor_copy(m).wait_recv()
        finish(peer(m), frecv[m - 1, 0], frecv[m - 1, 1])

    for i in range(share):
        weight_copy(i).wait_send()
        twin_copy(i, parity).wait_send()
    for q in range(PIECES):
        for b in range(2):
            hidden_copy(q, b).wait_send()
            forward_copy(q, b, core).wait_send()
            part_copy(b, q).wait_send()
    for m in range(1, n):
        gram_copy(m).wait_send()
        factor_copy(m).wait_send()


def fast_shards(n, hidden, row_scale, key_value_weight, outlier, sketch_sign_flags):
    tok = hidden.shape[0]
    kblk, heads, per_head = key_value_weight.shape
    cols = heads * per_head
    groups = outlier.shape[0]
    retain = jnp.repeat((1 - outlier).astype(jnp.float32), per_head, axis=1)
    signs = (2 * sketch_sign_flags - 1).astype(jnp.float32).transpose(0, 1, 3, 2)
    f32 = jnp.float32
    any_spec = pl.BlockSpec(memory_space=pl.ANY)
    vmem = pl.BlockSpec(memory_space=pltpu.VMEM)
    dma = pltpu.SemaphoreType.DMA
    depth = kblk // 16
    left, right, _ = pl.pallas_call(
        functools.partial(kernel, n, groups, math.sqrt(tok * n)),
        out_shape=(
            jax.ShapeDtypeStruct((heads, tok, 128), jnp.bfloat16),
            jax.ShapeDtypeStruct((heads, 128, 128), f32),
            jax.ShapeDtypeStruct((kblk, heads, per_head), f32),
        ),
        in_specs=[any_spec, any_spec, vmem, vmem, vmem],
        out_specs=(vmem, vmem, any_spec),
        scratch_shapes=[
            pltpu.VMEM((2 * kblk, cols), jnp.bfloat16),
            pltpu.VMEM((2 * kblk, cols), jnp.bfloat16),
            pltpu.VMEM((2, depth, heads, per_head), f32),
            pltpu.VMEM((tok, 2 * kblk), f32),
            pltpu.VMEM((tok, 2 * kblk), f32),
            pltpu.VMEM((tok, cols), f32),
            pltpu.VMEM((tok, cols), f32),
            pltpu.VMEM((tok, cols), f32),
            pltpu.VMEM((heads, 2, 128, 128), f32),
            pltpu.VMEM((n - 1, 2, 128, 128), f32),
            pltpu.VMEM((2, 128, 128), f32),
            pltpu.VMEM((n - 1, 2, 128, 128), f32),
            dma((2,)),
            dma((2,)),
            dma((8,)),
            dma((8,)),
            dma((8,)),
            dma((8,)),
            dma((PIECES, 2)),
            dma((PIECES, 2)),
            dma((PIECES, 2)),
            dma((PIECES, 2)),
            dma((2, PIECES)),
            dma((2, PIECES)),
            dma((n - 1,)),
            dma((n - 1,)),
            dma((n - 1,)),
            dma((n - 1,)),
        ],
        compiler_params=pltpu.CompilerParams(
            collective_id=0, has_side_effects=True, vmem_limit_bytes=56 * 1024 * 1024
        ),
        cost_estimate=pl.CostEstimate(
            flops=6 * n * tok * kblk * cols, bytes_accessed=4 * n * tok * kblk, transcendentals=0
        ),
    )(hidden, key_value_weight, row_scale[:, None], retain, signs)
    return left, right


def shards(hidden, row_scale, key_value_weight, outlier, sketch_sign_flags):
    tok_rows = hidden.shape[0]
    head_count = key_value_weight.shape[1]
    kv_cols = key_value_weight.shape[2]
    head_dim = kv_cols // 2
    rank_cols = sketch_sign_flags.shape[3]
    group_count = outlier.shape[0]
    highest = lax.Precision.HIGHEST
    weight_piece = lax.all_gather(key_value_weight, "seq", axis=0, tiled=True)
    flat_piece = weight_piece.reshape(weight_piece.shape[0], head_count * kv_cols)
    projected_key_value = jnp.dot(hidden, flat_piece, precision=highest)
    projected_key_value = projected_key_value * row_scale[:, None]
    grouped_rows = projected_key_value.reshape(
        group_count, tok_rows // group_count, head_count, kv_cols
    )
    quantization_spacing = jnp.max(jnp.abs(grouped_rows), axis=1, keepdims=True) / 7.0 + 1e-06
    retain_mask = (1 - outlier).astype(jnp.float32)[:, None, :, None]
    residual_error = (
        retain_mask * jnp.sin(complete_cycle * grouped_rows / quantization_spacing)
    ).reshape(tok_rows, head_count, 2, head_dim)
    sign_matrix = (2 * sketch_sign_flags - 1).astype(jnp.float32)
    sketch = jnp.einsum("thec,heck->thek", residual_error, sign_matrix, precision=highest)
    for iteration in range(ITERS):
        local_gram = jnp.einsum("thek,theq->hekq", sketch, sketch, precision=highest)
        gram_matrix = lax.psum(local_gram, "seq")
        lower_factor = jnp.linalg.cholesky(gram_matrix)
        identity = jnp.broadcast_to(jnp.eye(rank_cols, dtype=gram_matrix.dtype), gram_matrix.shape)
        inverse_factor = jax.scipy.linalg.solve_triangular(lower_factor, identity, lower=True)
        basis_matrix = jnp.einsum("thek,heqk->theq", sketch, inverse_factor, precision=highest)
        local_coef = jnp.einsum("thec,theq->hecq", residual_error, basis_matrix, precision=highest)
        coefficient_rows = lax.psum(local_coef, "seq")
        if iteration + 1 < ITERS:
            sketch = jnp.einsum(
                "thec,hecq->theq", residual_error, coefficient_rows, precision=highest
            )
    root_length = math.sqrt(tok_rows * lax.axis_size("seq"))
    left = (
        (root_length * basis_matrix)
        .transpose(1, 0, 2, 3)
        .reshape(head_count, tok_rows, 2 * rank_cols)
        .astype(jnp.bfloat16)
    )
    right = (
        (coefficient_rows / root_length)
        .transpose(0, 2, 1, 3)
        .reshape(head_count, head_dim, 2 * rank_cols)
    )
    return (left, right)


def solution(mesh):
    def run(hidden, row_scale, key_value_weight, outlier, sketch_sign_flags):
        members = mesh.shape["seq"]
        heads = key_value_weight.shape[1] // mesh.shape["head"]
        fits = members == 4 and heads == members
        fits = fits and mesh.shape["head"] == 2 and mesh.shape["batch"] % 2 == 0
        chosen = functools.partial(fast_shards, members) if fits else shards
        return mapped(chosen)(hidden, row_scale, key_value_weight, outlier, sketch_sign_flags)

    def mapped(chosen):
        return jax.shard_map(
            chosen,
            mesh=mesh,
            in_specs=(
                P(("batch", "seq"), None),
                P(("batch", "seq")),
                P("seq", "head", None),
                P(("batch", "seq"), "head"),
                P("head", None, None, None),
            ),
            out_specs=(P("head", ("batch", "seq"), None), P(("batch", "head"), None, None)),
            check_vma=False,
        )

    return run
```

```python
import functools
import math

import jax
import jax.numpy as jnp
import numpy as np
from jax import lax
from jax.experimental import pallas as pl
from jax.experimental.pallas import tpu as pltpu
from jax.sharding import PartitionSpec as P

ITERS = 2
BLOCK = 4
MESH = pl.DeviceIdType.MESH
HIGHEST = lax.Precision.HIGHEST

complete_cycle = 2.0 * math.pi


def sine_coefficients(terms=8):
    nodes = np.cos(np.pi * (np.arange(400) + 0.5) / 400)
    r = 0.25 + 0.25 * nodes
    values = np.sin(2 * np.pi * r) / r
    square = r * r
    scaled = square * 8 - 1
    fit = np.polynomial.chebyshev.chebfit(scaled, values, terms - 1)
    series = np.polynomial.chebyshev.cheb2poly(fit)
    power = np.zeros(1)
    for c in series[::-1]:
        power = np.polynomial.polynomial.polyadd(
            np.polynomial.polynomial.polymul(power, [-1.0, 8.0]), [c]
        )
    return [float(c) for c in power[:terms]]


SINE = sine_coefficients()


def sine_of_cycles(x):
    r = x - jnp.round(x)
    s = r * r
    total = jnp.full_like(s, SINE[-1])
    for c in SINE[-2::-1]:
        total = total * s + c
    return total * r


def split(x):
    hi = x.astype(jnp.bfloat16)
    return hi, (x - hi.astype(jnp.float32)).astype(jnp.bfloat16)


def dot(a, b):
    return jnp.dot(a, b, preferred_element_type=jnp.float32)


def dot_nt(a, b, precision=None):
    return lax.dot_general(
        a, b, (((1,), (1,)), ((), ())), precision=precision, preferred_element_type=jnp.float32
    )


def inverse_factors(grams):
    k = grams[0].shape[0]
    sub = lax.broadcasted_iota(jnp.int32, (k, 2 * k), 0)
    lane = lax.broadcasted_iota(jnp.int32, (k, 2 * k), 1)
    start = []
    for gram in grams:
        eye = (sub[:, :k] == lane[:, :k]).astype(jnp.float32)
        start.append(jnp.concatenate([gram, eye], axis=1))

    def step(i, state):
        at = i * BLOCK
        out = []
        for x in state:
            rows, columns = [], []
            for t in range(BLOCK):
                rows.append(jnp.sum(jnp.where(sub == at + t, x, 0.0), axis=0, keepdims=True))
                picked = jnp.sum(jnp.where(lane == at + t, x, 0.0), axis=1, keepdims=True)
                columns.append(jnp.broadcast_to(picked, x.shape))
            for t in range(BLOCK):
                entry = [
                    jnp.sum(jnp.where(sub == at + u, columns[t], 0.0), axis=0, keepdims=True)
                    for u in range(t, BLOCK)
                ]
                inverse = 1.0 / entry[0]
                factor = jnp.where(sub > at + t, columns[t] * inverse, 0.0)
                for u in range(t + 1, BLOCK):
                    columns[u] = columns[u] - factor * entry[u - t]
                    rows[u] = rows[u] - (entry[u - t] * inverse) * rows[t]
                x = x - factor * rows[t]
            out.append(x)
        return tuple(out)

    done = lax.fori_loop(0, k // BLOCK, step, tuple(start))
    result = []
    for x in done:
        pivots = jnp.sum(jnp.where(sub == lane, x, 0.0), axis=1, keepdims=True)
        result.append(x[:, k:] * lax.rsqrt(pivots))
    return result


def kernel(
    n, groups, root, hid, weight, scale, retain, signs, left, right,
    whi, wlo, stage, own, got, part, sums, res, gsend, grecv, factors, frecv,
    wsem, osem, hsend, hrecv, fsend, frsem, psend, precv, gs, gr, ms, mr,
):
    me = lax.axis_index("seq")
    core = lax.axis_index("head")
    tok, kblk = own.shape
    cols = whi.shape[1]
    half = tok // 2
    pieces = 2
    chunk = half // pieces
    heads = cols // 256

    across = {1: me + 1 - 2 * lax.rem(me, 2), 2: lax.rem(me + 2, n), 3: n - 1 - me}

    def peer(m):
        return across[m]

    barrier = pltpu.get_barrier_semaphore()
    for r in range(1, n):
        pl.semaphore_signal(barrier, inc=1, device_id={"seq": peer(r)}, device_id_type=MESH)
    pl.semaphore_signal(barrier, inc=1, device_id={"head": 1 - core}, device_id_type=MESH)

    load_own = pltpu.make_async_copy(
        hid.at[:, pl.ds(pl.multiple_of(me * kblk, 128), kblk)], own, osem
    )
    load_own.start()
    depth = stage.shape[1]
    loads = kblk // depth

    def load_weight(i):
        slot = lax.rem(i, 2)
        return pltpu.make_async_copy(
            weight.at[pl.ds(pl.multiple_of(i * depth, depth), depth)], stage.at[slot], wsem.at[slot]
        )

    load_weight(0).start()
    pl.semaphore_wait(barrier, n)

    def rows_of(which, q):
        return pl.ds(pl.multiple_of(which * half + q * chunk, chunk), chunk)

    def hidden_copy(q, m):
        p = peer(m)
        return pltpu.make_async_remote_copy(
            src_ref=hid.at[rows_of(core, q), pl.ds(pl.multiple_of(p * kblk, 128), kblk)],
            dst_ref=got.at[m - 1, rows_of(core, q)],
            send_sem=hsend.at[q, m - 1],
            recv_sem=hrecv.at[q, m - 1],
            device_id={"seq": p},
            device_id_type=MESH,
        )

    def hidden_arrival(q, m):
        return pltpu.make_async_remote_copy(
            src_ref=got.at[m - 1, rows_of(core, q)],
            dst_ref=got.at[m - 1, rows_of(core, q)],
            send_sem=hsend.at[q, m - 1],
            recv_sem=hrecv.at[q, m - 1],
            device_id={"seq": peer(m)},
            device_id_type=MESH,
        )

    def forward_copy(q, m, which):
        return pltpu.make_async_remote_copy(
            src_ref=got.at[m - 1, rows_of(which, q)],
            dst_ref=got.at[m - 1, rows_of(which, q)],
            send_sem=fsend.at[q, m - 1],
            recv_sem=frsem.at[q, m - 1],
            device_id={"head": 1 - core},
            device_id_type=MESH,
        )

    def via_copy(which, q):
        return pltpu.make_async_remote_copy(
            src_ref=part.at[2, rows_of(which, q)],
            dst_ref=sums.at[2, rows_of(which, q)],
            send_sem=psend.at[2, which, q],
            recv_sem=precv.at[2, which, q],
            device_id={"seq": which * across[1] + (1 - which) * across[2]},
            device_id_type=MESH,
        )

    def part_copy(slot, which, q):
        return pltpu.make_async_remote_copy(
            src_ref=part.at[slot, rows_of(which, q)],
            dst_ref=sums.at[slot, rows_of(which, q)],
            send_sem=psend.at[slot, which, q],
            recv_sem=precv.at[slot, which, q],
            device_id={"seq": (1 - slot) * across[1] + slot * across[2]},
            device_id_type=MESH,
        )

    for q in range(pieces):
        for m in (3, 1, 2):
            hidden_copy(q, m).start()

    def project(src, dst, rows):
        hi, lo = split(src[rows])

        def tile(t, carry):
            c = pl.ds(pl.multiple_of(t * 256, 256), 256)
            w = whi[:, c]
            dst[rows, c] = dot(hi, w) + dot(lo, w) + dot(hi, wlo[:, c])
            return carry

        lax.fori_loop(0, cols // 256, tile, 0)

    def split_weight(i, carry):
        @pl.when(i + 1 < loads)
        def _():
            load_weight(i + 1).start()

        load_weight(i).wait()
        rows = pl.ds(pl.multiple_of(i * depth, depth), depth)
        for h in range(heads):
            hi, lo = split(stage[lax.rem(i, 2), :, h, :])
            whi[rows, h * 256 : (h + 1) * 256] = hi
            wlo[rows, h * 256 : (h + 1) * 256] = lo
        return carry

    lax.fori_loop(0, loads, split_weight, 0)
    load_own.wait()

    def own_step(i, carry):
        project(own, res, pl.ds(pl.multiple_of(i * chunk, chunk), chunk))
        return carry

    lax.fori_loop(0, tok // chunk, own_step, 0)

    def pass_on(i):
        q = i // 2
        which = lax.rem(core + i, 2)
        rows = rows_of(which, q)
        via_copy(which, q).wait_recv()
        part[which, rows] = part[which, rows] + sums[2, rows]
        part_copy(which, which, q).start()

    def step(i, carry):
        q = i // 2
        which = lax.rem(core + i, 2)
        for m in (3, 1, 2):

            @pl.when(lax.rem(i, 2) == 0)
            def _():
                hidden_arrival(q, m).wait_recv()
                forward_copy(q, m, core).start()

            @pl.when(lax.rem(i, 2) == 1)
            def _():
                forward_copy(q, m, 1 - core).wait_recv()

            project(got.at[m - 1], part.at[m - 1], rows_of(which, q))
            if m == 3:
                via_copy(which, q).start()
        part_copy(1 - which, which, q).start()

        @pl.when(i > 0)
        def _():
            pass_on(i - 1)

        return carry

    lax.fori_loop(0, 2 * pieces, step, 0)
    pass_on(2 * pieces - 1)

    group = tok // groups
    per = chunk // group

    def residual(i, carry):
        q = i // 2
        which = lax.rem(core + i, 2)
        for slot in range(2):
            part_copy(slot, which, q).wait_recv()
        for g in range(per):
            at = (which * pieces + q) * per + g
            rows = pl.ds(pl.multiple_of(at * group, group), group)
            kv = res[rows]
            for slot in range(2):
                kv = kv + sums[slot, rows]
            kv = kv * scale[rows]
            spacing = jnp.max(jnp.abs(kv), axis=0, keepdims=True) / 7.0 + 1e-06
            res[rows] = retain[pl.ds(at, 1)] * sine_of_cycles(kv * (1.0 / spacing))
        rows = rows_of(which, q)

        def square(h, carry):
            for e in range(2):
                hi, lo = split(res[rows, pl.ds(pl.multiple_of(h * 256 + e * 128, 128), 128)])
                both = jnp.concatenate([hi, lo], axis=1)
                g = lax.dot_general(
                    both, both, (((0,), (0,)), ((), ())), preferred_element_type=jnp.float32
                )
                gsend[h, e] += g[:128, :128] + (g[:128, 128:] + g[128:, :128])
            return carry

        return lax.fori_loop(0, heads, square, carry)

    gsend[...] = jnp.zeros_like(gsend)
    lax.fori_loop(0, 2 * pieces, residual, 0)

    def gram_copy(m):
        return pltpu.make_async_remote_copy(
            src_ref=gsend.at[peer(m)],
            dst_ref=grecv.at[m - 1],
            send_sem=gs.at[m - 1],
            recv_sem=gr.at[m - 1],
            device_id={"seq": peer(m)},
            device_id_type=MESH,
        )

    for m in (3, 1, 2):
        gram_copy(m).start()
    for m in range(1, n):
        gram_copy(m).wait_recv()

    total = [gsend[me, e] for e in range(2)]
    for slot in range(n - 1):
        total = [total[e] + grecv[slot, e] for e in range(2)]
    sketch = [signs[me, e] for e in range(2)]
    for iteration in range(ITERS):
        product = [jnp.dot(sketch[e], total[e], precision=HIGHEST) for e in range(2)]
        inverse = inverse_factors([dot_nt(product[e], sketch[e], HIGHEST) for e in range(2)])
        coefficient = [jnp.dot(inverse[e], product[e], precision=HIGHEST) for e in range(2)]
        if iteration + 1 < ITERS:
            sketch = coefficient
        else:
            sketch = [jnp.dot(inverse[e], sketch[e], precision=HIGHEST) for e in range(2)]
    rank = sketch[0].shape[0]
    for e in range(2):
        factors[0, e * rank : (e + 1) * rank] = sketch[e] * root
    factors[1] = jnp.concatenate(coefficient, axis=0).T * (1.0 / root)

    def factor_copy(m):
        return pltpu.make_async_remote_copy(
            src_ref=factors,
            dst_ref=frecv.at[m - 1],
            send_sem=ms.at[m - 1],
            recv_sem=mr.at[m - 1],
            device_id={"seq": peer(m)},
            device_id_type=MESH,
        )

    for m in (3, 1, 2):
        factor_copy(m).start()

    def finish(h, matrix, coefficient_rows):
        zero = jnp.zeros((rank, 128), jnp.float32)
        block = jnp.concatenate(
            [
                jnp.concatenate([matrix[:rank], zero], axis=1),
                jnp.concatenate([zero, matrix[rank:]], axis=1),
            ],
            axis=0,
        )
        mhi, mlo = split(block)
        hi, lo = split(res[:, pl.ds(pl.multiple_of(h * 256, 256), 256)])
        value = dot_nt(hi, mhi) + (dot_nt(lo, mhi) + dot_nt(hi, mlo))
        left[h] = value.astype(jnp.bfloat16)
        right[h] = coefficient_rows

    finish(me, factors[0], factors[1])
    for m in range(1, n):
        factor_copy(m).wait_recv()
        finish(peer(m), frecv[m - 1, 0], frecv[m - 1, 1])

    for q in range(pieces):
        for m in range(1, n):
            hidden_copy(q, m).wait_send()
            forward_copy(q, m, core).wait_send()
        for which in range(2):
            via_copy(which, q).wait_send()
            for slot in range(2):
                part_copy(slot, which, q).wait_send()
    for m in range(1, n):
        gram_copy(m).wait_send()
        factor_copy(m).wait_send()


def fast_shards(n, hidden, row_scale, key_value_weight, outlier, sketch_sign_flags):
    tok = hidden.shape[0]
    kblk, heads, per_head = key_value_weight.shape
    cols = heads * per_head
    groups = outlier.shape[0]
    retain = jnp.repeat((1 - outlier).astype(jnp.float32), per_head, axis=1)
    signs = (2 * sketch_sign_flags - 1).astype(jnp.float32).transpose(0, 1, 3, 2)
    f32 = jnp.float32
    any_spec = pl.BlockSpec(memory_space=pl.ANY)
    vmem = pl.BlockSpec(memory_space=pltpu.VMEM)
    dma = pltpu.SemaphoreType.DMA
    left, right = pl.pallas_call(
        functools.partial(kernel, n, groups, math.sqrt(tok * n)),
        out_shape=(
            jax.ShapeDtypeStruct((heads, tok, 128), jnp.bfloat16),
            jax.ShapeDtypeStruct((heads, 128, 128), f32),
        ),
        in_specs=[any_spec, any_spec, vmem, vmem, vmem],
        out_specs=(vmem, vmem),
        scratch_shapes=[
            pltpu.VMEM((kblk, cols), jnp.bfloat16),
            pltpu.VMEM((kblk, cols), jnp.bfloat16),
            pltpu.VMEM((2, math.gcd(kblk, 256), heads, per_head), f32),
            pltpu.VMEM((tok, kblk), f32),
            pltpu.VMEM((n - 1, tok, kblk), f32),
            pltpu.VMEM((n - 1, tok, cols), f32),
            pltpu.VMEM((n - 1, tok, cols), f32),
            pltpu.VMEM((tok, cols), f32),
            pltpu.VMEM((heads, 2, 128, 128), f32),
            pltpu.VMEM((n - 1, 2, 128, 128), f32),
            pltpu.VMEM((2, 128, 128), f32),
            pltpu.VMEM((n - 1, 2, 128, 128), f32),
            dma((2,)),
            dma,
            dma((2, n - 1)),
            dma((2, n - 1)),
            dma((2, n - 1)),
            dma((2, n - 1)),
            dma((n - 1, 2, 2)),
            dma((n - 1, 2, 2)),
            dma((n - 1,)),
            dma((n - 1,)),
            dma((n - 1,)),
            dma((n - 1,)),
        ],
        compiler_params=pltpu.CompilerParams(
            collective_id=0, has_side_effects=True, vmem_limit_bytes=56 * 1024 * 1024
        ),
        cost_estimate=pl.CostEstimate(
            flops=6 * n * tok * kblk * cols, bytes_accessed=4 * n * tok * kblk, transcendentals=0
        ),
    )(hidden, key_value_weight, row_scale[:, None], retain, signs)
    return left, right


def shards(hidden, row_scale, key_value_weight, outlier, sketch_sign_flags):
    tok_rows = hidden.shape[0]
    head_count = key_value_weight.shape[1]
    kv_cols = key_value_weight.shape[2]
    head_dim = kv_cols // 2
    rank_cols = sketch_sign_flags.shape[3]
    group_count = outlier.shape[0]
    highest = lax.Precision.HIGHEST
    weight_piece = lax.all_gather(key_value_weight, "seq", axis=0, tiled=True)
    flat_piece = weight_piece.reshape(weight_piece.shape[0], head_count * kv_cols)
    projected_key_value = jnp.dot(hidden, flat_piece, precision=highest)
    projected_key_value = projected_key_value * row_scale[:, None]
    grouped_rows = projected_key_value.reshape(
        group_count, tok_rows // group_count, head_count, kv_cols
    )
    quantization_spacing = jnp.max(jnp.abs(grouped_rows), axis=1, keepdims=True) / 7.0 + 1e-06
    retain_mask = (1 - outlier).astype(jnp.float32)[:, None, :, None]
    residual_error = (
        retain_mask * jnp.sin(complete_cycle * grouped_rows / quantization_spacing)
    ).reshape(tok_rows, head_count, 2, head_dim)
    sign_matrix = (2 * sketch_sign_flags - 1).astype(jnp.float32)
    sketch = jnp.einsum("thec,heck->thek", residual_error, sign_matrix, precision=highest)
    for iteration in range(ITERS):
        local_gram = jnp.einsum("thek,theq->hekq", sketch, sketch, precision=highest)
        gram_matrix = lax.psum(local_gram, "seq")
        lower_factor = jnp.linalg.cholesky(gram_matrix)
        identity = jnp.broadcast_to(jnp.eye(rank_cols, dtype=gram_matrix.dtype), gram_matrix.shape)
        inverse_factor = jax.scipy.linalg.solve_triangular(lower_factor, identity, lower=True)
        basis_matrix = jnp.einsum("thek,heqk->theq", sketch, inverse_factor, precision=highest)
        local_coef = jnp.einsum("thec,theq->hecq", residual_error, basis_matrix, precision=highest)
        coefficient_rows = lax.psum(local_coef, "seq")
        if iteration + 1 < ITERS:
            sketch = jnp.einsum(
                "thec,hecq->theq", residual_error, coefficient_rows, precision=highest
            )
    root_length = math.sqrt(tok_rows * lax.axis_size("seq"))
    left = (
        (root_length * basis_matrix)
        .transpose(1, 0, 2, 3)
        .reshape(head_count, tok_rows, 2 * rank_cols)
        .astype(jnp.bfloat16)
    )
    right = (
        (coefficient_rows / root_length)
        .transpose(0, 2, 1, 3)
        .reshape(head_count, head_dim, 2 * rank_cols)
    )
    return (left, right)


def solution(mesh):
    def run(hidden, row_scale, key_value_weight, outlier, sketch_sign_flags):
        members = mesh.shape["seq"]
        heads = key_value_weight.shape[1] // mesh.shape["head"]
        fits = members == 4 and heads == members and mesh.shape["head"] == 2
        chosen = functools.partial(fast_shards, members) if fits else shards
        return mapped(chosen)(hidden, row_scale, key_value_weight, outlier, sketch_sign_flags)

    def mapped(chosen):
        return jax.shard_map(
            chosen,
            mesh=mesh,
            in_specs=(
                P(("batch", "seq"), None),
                P(("batch", "seq")),
                P("seq", "head", None),
                P(("batch", "seq"), "head"),
                P("head", None, None, None),
            ),
            out_specs=(P("head", ("batch", "seq"), None), P(("batch", "head"), None, None)),
            check_vma=False,
        )

    return run
```

```python
import functools
import math

import jax
import jax.numpy as jnp
import numpy as np
from jax import lax
from jax.experimental import pallas as pl
from jax.experimental.pallas import tpu as pltpu
from jax.sharding import PartitionSpec as P

ITERS = 2
BLOCK = 8
MESH = pl.DeviceIdType.MESH
HIGHEST = lax.Precision.HIGHEST

complete_cycle = 2.0 * math.pi


def sine_coefficients(terms=8):
    nodes = np.cos(np.pi * (np.arange(400) + 0.5) / 400)
    r = 0.25 + 0.25 * nodes
    values = np.sin(2 * np.pi * r) / r
    square = r * r
    scaled = square * 8 - 1
    fit = np.polynomial.chebyshev.chebfit(scaled, values, terms - 1)
    series = np.polynomial.chebyshev.cheb2poly(fit)
    power = np.zeros(1)
    for c in series[::-1]:
        power = np.polynomial.polynomial.polyadd(
            np.polynomial.polynomial.polymul(power, [-1.0, 8.0]), [c]
        )
    return [float(c) for c in power[:terms]]


SINE = sine_coefficients()


def sine_of_cycles(x):
    r = x - jnp.round(x)
    s = r * r
    total = jnp.full_like(s, SINE[-1])
    for c in SINE[-2::-1]:
        total = total * s + c
    return total * r


def split(x):
    hi = x.astype(jnp.bfloat16)
    return hi, (x - hi.astype(jnp.float32)).astype(jnp.bfloat16)


def dot(a, b):
    return jnp.dot(a, b, preferred_element_type=jnp.float32)


def dot_nt(a, b, precision=None):
    return lax.dot_general(
        a, b, (((1,), (1,)), ((), ())), precision=precision, preferred_element_type=jnp.float32
    )


def inverse_factors(grams):
    k = grams[0].shape[0]
    sub = lax.broadcasted_iota(jnp.int32, (k, 2 * k), 0)
    lane = lax.broadcasted_iota(jnp.int32, (k, 2 * k), 1)
    start = []
    for gram in grams:
        eye = (sub[:, :k] == lane[:, :k]).astype(jnp.float32)
        start.append(jnp.concatenate([gram, eye], axis=1))

    def step(i, state):
        at = i * BLOCK
        out = []
        for x in state:
            rows, columns = [], []
            for t in range(BLOCK):
                rows.append(jnp.sum(jnp.where(sub == at + t, x, 0.0), axis=0, keepdims=True))
                picked = jnp.sum(jnp.where(lane == at + t, x, 0.0), axis=1, keepdims=True)
                columns.append(jnp.broadcast_to(picked, x.shape))
            for t in range(BLOCK):
                entry = [
                    jnp.sum(jnp.where(sub == at + u, columns[t], 0.0), axis=0, keepdims=True)
                    for u in range(t, BLOCK)
                ]
                inverse = 1.0 / entry[0]
                factor = jnp.where(sub > at + t, columns[t] * inverse, 0.0)
                for u in range(t + 1, BLOCK):
                    columns[u] = columns[u] - factor * entry[u - t]
                    rows[u] = rows[u] - (entry[u - t] * inverse) * rows[t]
                x = x - factor * rows[t]
            out.append(x)
        return tuple(out)

    done = lax.fori_loop(0, k // BLOCK, step, tuple(start))
    result = []
    for x in done:
        pivots = jnp.sum(jnp.where(sub == lane, x, 0.0), axis=1, keepdims=True)
        result.append(x[:, k:] * lax.rsqrt(pivots))
    return result


def kernel(
    n, groups, root, hid, weight, scale, retain, signs, left, right,
    whi, wlo, stage, own, got, part, sums, res, gsend, grecv, factors, frecv,
    wsem, osem, hsend, hrecv, fsend, frsem, psend, precv, gs, gr, ms, mr,
):
    me = lax.axis_index("seq")
    core = lax.axis_index("head")
    tok, kblk = own.shape
    cols = whi.shape[1]
    half = tok // 2
    pieces = 2
    chunk = half // pieces
    heads = cols // 256

    across = {1: me + 1 - 2 * lax.rem(me, 2), 2: lax.rem(me + 2, n), 3: n - 1 - me}

    def peer(m):
        return across[m]

    barrier = pltpu.get_barrier_semaphore()
    for r in range(1, n):
        pl.semaphore_signal(barrier, inc=1, device_id={"seq": peer(r)}, device_id_type=MESH)
    pl.semaphore_signal(barrier, inc=1, device_id={"head": 1 - core}, device_id_type=MESH)

    load_own = pltpu.make_async_copy(
        hid.at[:, pl.ds(pl.multiple_of(me * kblk, 128), kblk)], own, osem
    )
    load_own.start()
    depth = stage.shape[1]
    loads = kblk // depth

    def load_weight(i):
        slot = lax.rem(i, 2)
        return pltpu.make_async_copy(
            weight.at[pl.ds(pl.multiple_of(i * depth, depth), depth)], stage.at[slot], wsem.at[slot]
        )

    load_weight(0).start()
    pl.semaphore_wait(barrier, n)

    def rows_of(which, q):
        return pl.ds(pl.multiple_of(which * half + q * chunk, chunk), chunk)

    def hidden_copy(q, m):
        p = peer(m)
        return pltpu.make_async_remote_copy(
            src_ref=hid.at[rows_of(core, q), pl.ds(pl.multiple_of(p * kblk, 128), kblk)],
            dst_ref=got.at[m - 1, rows_of(core, q)],
            send_sem=hsend.at[q, m - 1],
            recv_sem=hrecv.at[q, m - 1],
            device_id={"seq": p},
            device_id_type=MESH,
        )

    def hidden_arrival(q, m):
        return pltpu.make_async_remote_copy(
            src_ref=got.at[m - 1, rows_of(core, q)],
            dst_ref=got.at[m - 1, rows_of(core, q)],
            send_sem=hsend.at[q, m - 1],
            recv_sem=hrecv.at[q, m - 1],
            device_id={"seq": peer(m)},
            device_id_type=MESH,
        )

    def forward_copy(q, m, which):
        return pltpu.make_async_remote_copy(
            src_ref=got.at[m - 1, rows_of(which, q)],
            dst_ref=got.at[m - 1, rows_of(which, q)],
            send_sem=fsend.at[q, m - 1],
            recv_sem=frsem.at[q, m - 1],
            device_id={"head": 1 - core},
            device_id_type=MESH,
        )

    def via_copy(which, q):
        return pltpu.make_async_remote_copy(
            src_ref=part.at[2, rows_of(which, q)],
            dst_ref=sums.at[2, rows_of(which, q)],
            send_sem=psend.at[2, which, q],
            recv_sem=precv.at[2, which, q],
            device_id={"seq": which * across[1] + (1 - which) * across[2]},
            device_id_type=MESH,
        )

    def part_copy(slot, which, q):
        return pltpu.make_async_remote_copy(
            src_ref=part.at[slot, rows_of(which, q)],
            dst_ref=sums.at[slot, rows_of(which, q)],
            send_sem=psend.at[slot, which, q],
            recv_sem=precv.at[slot, which, q],
            device_id={"seq": (1 - slot) * across[1] + slot * across[2]},
            device_id_type=MESH,
        )

    for q in range(pieces):
        for m in (3, 1, 2):
            hidden_copy(q, m).start()

    def project(src, dst, rows):
        hi, lo = split(src[rows])

        def tile(t, carry):
            c = pl.ds(pl.multiple_of(t * 256, 256), 256)
            w = whi[:, c]
            dst[rows, c] = dot(hi, w) + dot(lo, w) + dot(hi, wlo[:, c])
            return carry

        lax.fori_loop(0, cols // 256, tile, 0)

    def split_weight(i, carry):
        @pl.when(i + 1 < loads)
        def _():
            load_weight(i + 1).start()

        load_weight(i).wait()
        rows = pl.ds(pl.multiple_of(i * depth, depth), depth)
        for h in range(heads):
            hi, lo = split(stage[lax.rem(i, 2), :, h, :])
            whi[rows, h * 256 : (h + 1) * 256] = hi
            wlo[rows, h * 256 : (h + 1) * 256] = lo
        return carry

    lax.fori_loop(0, loads, split_weight, 0)
    load_own.wait()

    def own_step(i, carry):
        project(own, res, pl.ds(pl.multiple_of(i * chunk, chunk), chunk))
        return carry

    lax.fori_loop(0, tok // chunk, own_step, 0)

    def pass_on(i):
        q = i // 2
        which = lax.rem(core + i, 2)
        rows = rows_of(which, q)
        via_copy(which, q).wait_recv()
        part[which, rows] = part[which, rows] + sums[2, rows]
        part_copy(which, which, q).start()

    def step(i, carry):
        q = i // 2
        which = lax.rem(core + i, 2)
        for m in (3, 1, 2):

            @pl.when(lax.rem(i, 2) == 0)
            def _():
                hidden_arrival(q, m).wait_recv()
                forward_copy(q, m, core).start()

            @pl.when(lax.rem(i, 2) == 1)
            def _():
                forward_copy(q, m, 1 - core).wait_recv()

            project(got.at[m - 1], part.at[m - 1], rows_of(which, q))
            if m == 3:
                via_copy(which, q).start()
        part_copy(1 - which, which, q).start()

        @pl.when(i > 0)
        def _():
            pass_on(i - 1)

        return carry

    lax.fori_loop(0, 2 * pieces, step, 0)
    pass_on(2 * pieces - 1)

    group = tok // groups
    per = chunk // group

    def residual(i, carry):
        which = i // pieces
        q = lax.rem(i, pieces)
        for slot in range(2):
            part_copy(slot, which, q).wait_recv()
        for g in range(per):
            at = i * per + g
            rows = pl.ds(pl.multiple_of(at * group, group), group)
            kv = res[rows]
            for slot in range(2):
                kv = kv + sums[slot, rows]
            kv = kv * scale[rows]
            spacing = jnp.max(jnp.abs(kv), axis=0, keepdims=True) / 7.0 + 1e-06
            res[rows] = retain[pl.ds(at, 1)] * sine_of_cycles(kv * (1.0 / spacing))
        return carry

    lax.fori_loop(0, 2 * pieces, residual, 0)

    def square(h, carry):
        for e in range(2):
            hi, lo = split(res[:, pl.ds(pl.multiple_of(h * 256 + e * 128, 128), 128)])
            both = jnp.concatenate([hi, lo], axis=1)
            g = lax.dot_general(
                both, both, (((0,), (0,)), ((), ())), preferred_element_type=jnp.float32
            )
            gsend[h, e] = g[:128, :128] + (g[:128, 128:] + g[128:, :128])
        return carry

    lax.fori_loop(0, heads, square, 0)

    def gram_copy(m):
        return pltpu.make_async_remote_copy(
            src_ref=gsend.at[peer(m)],
            dst_ref=grecv.at[m - 1],
            send_sem=gs.at[m - 1],
            recv_sem=gr.at[m - 1],
            device_id={"seq": peer(m)},
            device_id_type=MESH,
        )

    for m in (3, 1, 2):
        gram_copy(m).start()
    for m in range(1, n):
        gram_copy(m).wait_recv()

    total = [gsend[me, e] for e in range(2)]
    for slot in range(n - 1):
        total = [total[e] + grecv[slot, e] for e in range(2)]
    sketch = [signs[me, e] for e in range(2)]
    for iteration in range(ITERS):
        product = [jnp.dot(sketch[e], total[e], precision=HIGHEST) for e in range(2)]
        inverse = inverse_factors([dot_nt(product[e], sketch[e], HIGHEST) for e in range(2)])
        coefficient = [jnp.dot(inverse[e], product[e], precision=HIGHEST) for e in range(2)]
        if iteration + 1 < ITERS:
            sketch = coefficient
        else:
            sketch = [jnp.dot(inverse[e], sketch[e], precision=HIGHEST) for e in range(2)]
    rank = sketch[0].shape[0]
    for e in range(2):
        factors[0, e * rank : (e + 1) * rank] = sketch[e] * root
    factors[1] = jnp.concatenate(coefficient, axis=0).T * (1.0 / root)

    def factor_copy(m):
        return pltpu.make_async_remote_copy(
            src_ref=factors,
            dst_ref=frecv.at[m - 1],
            send_sem=ms.at[m - 1],
            recv_sem=mr.at[m - 1],
            device_id={"seq": peer(m)},
            device_id_type=MESH,
        )

    for m in (3, 1, 2):
        factor_copy(m).start()

    def finish(h, matrix, coefficient_rows):
        zero = jnp.zeros((rank, 128), jnp.float32)
        block = jnp.concatenate(
            [
                jnp.concatenate([matrix[:rank], zero], axis=1),
                jnp.concatenate([zero, matrix[rank:]], axis=1),
            ],
            axis=0,
        )
        mhi, mlo = split(block)
        hi, lo = split(res[:, pl.ds(pl.multiple_of(h * 256, 256), 256)])
        value = dot_nt(hi, mhi) + (dot_nt(lo, mhi) + dot_nt(hi, mlo))
        left[h] = value.astype(jnp.bfloat16)
        right[h] = coefficient_rows

    finish(me, factors[0], factors[1])
    for m in range(1, n):
        factor_copy(m).wait_recv()
        finish(peer(m), frecv[m - 1, 0], frecv[m - 1, 1])

    for q in range(pieces):
        for m in range(1, n):
            hidden_copy(q, m).wait_send()
            forward_copy(q, m, core).wait_send()
        for which in range(2):
            via_copy(which, q).wait_send()
            for slot in range(2):
                part_copy(slot, which, q).wait_send()
    for m in range(1, n):
        gram_copy(m).wait_send()
        factor_copy(m).wait_send()


def fast_shards(n, hidden, row_scale, key_value_weight, outlier, sketch_sign_flags):
    tok = hidden.shape[0]
    kblk, heads, per_head = key_value_weight.shape
    cols = heads * per_head
    groups = outlier.shape[0]
    retain = jnp.repeat((1 - outlier).astype(jnp.float32), per_head, axis=1)
    signs = (2 * sketch_sign_flags - 1).astype(jnp.float32).transpose(0, 1, 3, 2)
    f32 = jnp.float32
    any_spec = pl.BlockSpec(memory_space=pl.ANY)
    vmem = pl.BlockSpec(memory_space=pltpu.VMEM)
    dma = pltpu.SemaphoreType.DMA
    left, right = pl.pallas_call(
        functools.partial(kernel, n, groups, math.sqrt(tok * n)),
        out_shape=(
            jax.ShapeDtypeStruct((heads, tok, 128), jnp.bfloat16),
            jax.ShapeDtypeStruct((heads, 128, 128), f32),
        ),
        in_specs=[any_spec, any_spec, vmem, vmem, vmem],
        out_specs=(vmem, vmem),
        scratch_shapes=[
            pltpu.VMEM((kblk, cols), jnp.bfloat16),
            pltpu.VMEM((kblk, cols), jnp.bfloat16),
            pltpu.VMEM((2, math.gcd(kblk, 256), heads, per_head), f32),
            pltpu.VMEM((tok, kblk), f32),
            pltpu.VMEM((n - 1, tok, kblk), f32),
            pltpu.VMEM((n - 1, tok, cols), f32),
            pltpu.VMEM((n - 1, tok, cols), f32),
            pltpu.VMEM((tok, cols), f32),
            pltpu.VMEM((heads, 2, 128, 128), f32),
            pltpu.VMEM((n - 1, 2, 128, 128), f32),
            pltpu.VMEM((2, 128, 128), f32),
            pltpu.VMEM((n - 1, 2, 128, 128), f32),
            dma((2,)),
            dma,
            dma((2, n - 1)),
            dma((2, n - 1)),
            dma((2, n - 1)),
            dma((2, n - 1)),
            dma((n - 1, 2, 2)),
            dma((n - 1, 2, 2)),
            dma((n - 1,)),
            dma((n - 1,)),
            dma((n - 1,)),
            dma((n - 1,)),
        ],
        compiler_params=pltpu.CompilerParams(
            collective_id=0, has_side_effects=True, vmem_limit_bytes=56 * 1024 * 1024
        ),
        cost_estimate=pl.CostEstimate(
            flops=6 * n * tok * kblk * cols, bytes_accessed=4 * n * tok * kblk, transcendentals=0
        ),
    )(hidden, key_value_weight, row_scale[:, None], retain, signs)
    return left, right


def shards(hidden, row_scale, key_value_weight, outlier, sketch_sign_flags):
    tok_rows = hidden.shape[0]
    head_count = key_value_weight.shape[1]
    kv_cols = key_value_weight.shape[2]
    head_dim = kv_cols // 2
    rank_cols = sketch_sign_flags.shape[3]
    group_count = outlier.shape[0]
    highest = lax.Precision.HIGHEST
    weight_piece = lax.all_gather(key_value_weight, "seq", axis=0, tiled=True)
    flat_piece = weight_piece.reshape(weight_piece.shape[0], head_count * kv_cols)
    projected_key_value = jnp.dot(hidden, flat_piece, precision=highest)
    projected_key_value = projected_key_value * row_scale[:, None]
    grouped_rows = projected_key_value.reshape(
        group_count, tok_rows // group_count, head_count, kv_cols
    )
    quantization_spacing = jnp.max(jnp.abs(grouped_rows), axis=1, keepdims=True) / 7.0 + 1e-06
    retain_mask = (1 - outlier).astype(jnp.float32)[:, None, :, None]
    residual_error = (
        retain_mask * jnp.sin(complete_cycle * grouped_rows / quantization_spacing)
    ).reshape(tok_rows, head_count, 2, head_dim)
    sign_matrix = (2 * sketch_sign_flags - 1).astype(jnp.float32)
    sketch = jnp.einsum("thec,heck->thek", residual_error, sign_matrix, precision=highest)
    for iteration in range(ITERS):
        local_gram = jnp.einsum("thek,theq->hekq", sketch, sketch, precision=highest)
        gram_matrix = lax.psum(local_gram, "seq")
        lower_factor = jnp.linalg.cholesky(gram_matrix)
        identity = jnp.broadcast_to(jnp.eye(rank_cols, dtype=gram_matrix.dtype), gram_matrix.shape)
        inverse_factor = jax.scipy.linalg.solve_triangular(lower_factor, identity, lower=True)
        basis_matrix = jnp.einsum("thek,heqk->theq", sketch, inverse_factor, precision=highest)
        local_coef = jnp.einsum("thec,theq->hecq", residual_error, basis_matrix, precision=highest)
        coefficient_rows = lax.psum(local_coef, "seq")
        if iteration + 1 < ITERS:
            sketch = jnp.einsum(
                "thec,hecq->theq", residual_error, coefficient_rows, precision=highest
            )
    root_length = math.sqrt(tok_rows * lax.axis_size("seq"))
    left = (
        (root_length * basis_matrix)
        .transpose(1, 0, 2, 3)
        .reshape(head_count, tok_rows, 2 * rank_cols)
        .astype(jnp.bfloat16)
    )
    right = (
        (coefficient_rows / root_length)
        .transpose(0, 2, 1, 3)
        .reshape(head_count, head_dim, 2 * rank_cols)
    )
    return (left, right)


def solution(mesh):
    def run(hidden, row_scale, key_value_weight, outlier, sketch_sign_flags):
        members = mesh.shape["seq"]
        heads = key_value_weight.shape[1] // mesh.shape["head"]
        fits = members == 4 and heads == members and mesh.shape["head"] == 2
        chosen = functools.partial(fast_shards, members) if fits else shards
        return mapped(chosen)(hidden, row_scale, key_value_weight, outlier, sketch_sign_flags)

    def mapped(chosen):
        return jax.shard_map(
            chosen,
            mesh=mesh,
            in_specs=(
                P(("batch", "seq"), None),
                P(("batch", "seq")),
                P("seq", "head", None),
                P(("batch", "seq"), "head"),
                P("head", None, None, None),
            ),
            out_specs=(P("head", ("batch", "seq"), None), P(("batch", "head"), None, None)),
            check_vma=False,
        )

    return run
```
